32 devices in a mesh: mem: 16 (over z, y, x), lat: 2 (over core).
Axes of the slice: x: 2, y: 2, z: 4, core: 2. Of those that a mesh axis runs over, the one named last changes fastest.
Arguments:
- ensemble_height_winds: float32 [512, 3, 32, 256], P('mem', None, 'lat'), may hold values from -6 to 6
- obs_count: int32 [2, 16], P('lat'), may hold values from 16 to 128, as said below
- obs_cell: int32 [2, 16, 128], P('lat'), may hold values from 0 to 255
- obs_value: float32 [2, 16, 128], P('lat'), may hold values from -6 to 6
- obs_rinv: float32 [2, 16, 128], P('lat'), may hold values from 0.5 to 8
Outputs:
- analysis: float32 [2, 16, 512, 3, 256], P('lat', 'mem')
The draws below stay inside these ranges and needn't reach their ends.
Inputs may be any that keep to these rules, and one draw needn't show every extreme that they name: `obs_count`: each region's count is 128, 64, 32 or 16, and some region has 128.
All inputs are finite; a program needn't handle non-finite values.
Results may differ from the reference program's by a relative error of at most 0.011.
Values may be sent and summed in bfloat16 or wider, within the bound.
A program may use at most 64 MiB of HBM per device.

```python
import math
import jax
import jax.numpy as jnp
from jax import lax

ENSEMBLE_SIZE = 512
PATCH_EDGE_LEN = 16
PMAX = 128
NS_ITERS = 5
PATCH_POINTS = 256
NLAT = 32
NLON = 256
PATCH_DOWN = 2
PATCH_ACROSS = 16


def draw_obs_count(key, part):
    level_key = jax.random.fold_in(key, 11)
    spot_key = jax.random.fold_in(key, 23)
    level_ids = jax.random.randint(level_key, (PATCH_DOWN * PATCH_ACROSS,), 0, 4)
    divisor = jnp.take(jnp.array([1, 2, 4, 8], dtype=jnp.int32), level_ids)
    counts = PMAX // divisor
    chosen = jax.random.randint(spot_key, (), 0, PATCH_DOWN * PATCH_ACROSS)
    counts = jnp.where(jnp.arange(PATCH_DOWN * PATCH_ACROSS) == chosen, PMAX, counts)
    return counts.reshape(PATCH_DOWN, PATCH_ACROSS).astype(jnp.int32)


def place_ends(values, own_key, smallest, largest):
    place = [jax.random.randint(jax.random.fold_in(own_key, axis), (), 0, length) for axis, length in enumerate(values.shape)]
    widest = values.shape.index(max(values.shape))
    next_to = place[:widest] + [(place[widest] + 1) % values.shape[widest]] + place[widest + 1:]
    return values.at[tuple(place)].set(smallest).at[tuple(next_to)].set(largest)


def block_levels(stream_key, extent, cuts, least, largest):
    factor_of = 1.0
    for axis_at, parts in cuts:
        steps = jax.random.uniform(jax.random.fold_in(jax.random.fold_in(stream_key, 6), axis_at), (parts,), jnp.float32, least / len(cuts), largest / len(cuts))
        factor_of = factor_of * jnp.repeat(jnp.exp(steps), extent[axis_at] // parts).reshape((-1,) + (1,) * (len(extent) - 1 - axis_at))
    return factor_of


def scatter_about(stream_key, shape, width, bound, shards=(), kind=jnp.bfloat16):
    values = jax.random.normal(stream_key, shape, jnp.float32) * width
    if len(shards) > 0:
        values = block_levels(stream_key, shape, shards, -0.22, 0.18) * values
    return jnp.clip(values, min=-bound, max=bound).astype(kind)


def setup_inputs(seed: int = 0) -> dict:
    keys = jax.random.split(jax.random.key(seed), 6)
    return {
        "ensemble_height_winds": scatter_about(keys[0], (ENSEMBLE_SIZE, 3, NLAT, NLON), 0.5, 6.0, ((0, 16), (2, 2)), jnp.float32),
        "obs_count": draw_obs_count(jax.random.fold_in(keys[5], 71), 0),
        "obs_cell": place_ends(jax.random.randint(keys[2], (PATCH_DOWN, PATCH_ACROSS, PMAX), 0, PATCH_POINTS), jax.random.fold_in(keys[2], 1), 0, PATCH_POINTS - 1).astype(jnp.int32),
        "obs_value": scatter_about(keys[3], (PATCH_DOWN, PATCH_ACROSS, PMAX), 1.0, 6.0, ((0, 2),), jnp.float32),
        "obs_rinv": jnp.clip(jnp.exp(math.log(8.0) - 2.7725887 * jax.random.uniform(keys[4], (PATCH_DOWN, PATCH_ACROSS, PMAX), jnp.float32) ** block_levels(keys[4], (PATCH_DOWN, PATCH_ACROSS, PMAX), ((0, 2),), -0.2, 0.2)), 0.5, 8.0),
    }


GRAVITY = 1.0
DEPTH = 1.0
CORIOLIS = 0.25
TIME_STEP = 0.5
EDGE_WEIGHT = 0.6
CORNER_WEIGHT = 0.35
NEWTON_SCALE = 16.0

def tendency(padded):
    height = padded[..., 0, :, :]
    east_wind = padded[..., 1, :, :]
    north_wind = padded[..., 2, :, :]

    def along_x(quantity):
        return (quantity[..., 1:-1, 2:] - quantity[..., 1:-1, :-2]) * 0.5

    def along_y(quantity):
        return (quantity[..., 2:, 1:-1] - quantity[..., :-2, 1:-1]) * 0.5
    east_mid = east_wind[..., 1:-1, 1:-1]
    north_mid = north_wind[..., 1:-1, 1:-1]
    flux_x = (DEPTH + height) * east_wind
    flux_y = (DEPTH + height) * north_wind
    rate_height = -(along_x(flux_x) + along_y(flux_y))
    rate_east = -(east_mid * along_x(east_wind) + north_mid * along_y(east_wind)) + CORIOLIS * north_mid - GRAVITY * along_x(height)
    rate_north = -(east_mid * along_x(north_wind) + north_mid * along_y(north_wind)) - CORIOLIS * east_mid - GRAVITY * along_y(height)
    return jnp.stack([rate_height, rate_east, rate_north], axis=-3)

def explicit_integrator(gridded_numbers):

    def with_zeros(quantity):
        return jnp.pad(quantity, ((0, 0), (1, 1), (1, 1)))
    section_one = gridded_numbers + TIME_STEP * tendency(with_zeros(gridded_numbers))
    section_two = 0.75 * gridded_numbers + 0.25 * (section_one + TIME_STEP * tendency(with_zeros(section_one)))
    return gridded_numbers / 3.0 + 2.0 / 3.0 * (section_two + TIME_STEP * tendency(with_zeros(section_two)))

def make_block(equivalents, number, measured, precision):
    ensemble = equivalents.shape[0]
    centre = lax.optimization_barrier(jnp.mean(equivalents, axis=0))
    slot_ids = jnp.arange(equivalents.shape[1], dtype=jnp.int32)
    weight = jnp.where(slot_ids < number, jnp.sqrt(precision), 0.0)
    scaled = (weight[:, None] * (equivalents.T - centre[:, None]) / math.sqrt(ensemble - 1)).astype(jnp.bfloat16)
    misfit = weight * (measured - centre)
    summary = jnp.dot(misfit, scaled.astype(jnp.float32), precision=lax.Precision.HIGHEST)
    return jnp.concatenate([scaled, summary.astype(jnp.bfloat16)[None, :]], axis=0)

def centre_region(region):
    flat_state = region.reshape(region.shape[0], -1)
    ens_mean = lax.optimization_barrier(jnp.mean(flat_state, axis=0))
    return (ens_mean, (flat_state - ens_mean).astype(jnp.bfloat16))

def analyse(neighbourhood, ens_mean, deviations):
    ensemble = deviations.shape[0]
    obs_slots = neighbourhood.shape[2] - 1
    locality = [[CORNER_WEIGHT, EDGE_WEIGHT, CORNER_WEIGHT], [EDGE_WEIGHT, 1.0, EDGE_WEIGHT], [CORNER_WEIGHT, EDGE_WEIGHT, CORNER_WEIGHT]]
    gram_sum = jnp.zeros((ensemble, ensemble), jnp.float32)
    mean_drive = jnp.zeros((ensemble,), jnp.float32)
    for row_off in range(3):
        for col_off in range(3):
            factor = locality[row_off][col_off]
            scaled = neighbourhood[row_off, col_off, :obs_slots]
            gram_sum = gram_sum + factor * lax.dot_general(scaled, scaled, (((0,), (0,)), ((), ())), preferred_element_type=jnp.float32)
            mean_drive = mean_drive + factor * neighbourhood[row_off, col_off, obs_slots].astype(jnp.float32)
    identity = jnp.eye(ensemble, dtype=jnp.float32)
    root_half = ((identity + gram_sum) / NEWTON_SCALE).astype(jnp.bfloat16)
    root_inverse = identity.astype(jnp.bfloat16)
    for sweep in range(NS_ITERS):
        product = jnp.dot(root_inverse, root_half, preferred_element_type=jnp.float32)
        correction = (1.5 * identity - 0.5 * product).astype(jnp.bfloat16)
        root_half = jnp.dot(root_half, correction, preferred_element_type=jnp.float32).astype(jnp.bfloat16)
        root_inverse = jnp.dot(correction, root_inverse, preferred_element_type=jnp.float32).astype(jnp.bfloat16)
    inverse_full = root_inverse.astype(jnp.float32)
    inner_step = jnp.dot(inverse_full, mean_drive, precision=lax.Precision.HIGHEST)
    mean_weights = jnp.dot(inverse_full, inner_step, precision=lax.Precision.HIGHEST) / NEWTON_SCALE
    transform = (mean_weights[:, None] / math.sqrt(ensemble - 1) + inverse_full / math.sqrt(NEWTON_SCALE)).astype(jnp.bfloat16)
    return ens_mean + lax.dot_general(transform, deviations, (((0,), (0,)), ((), ())), preferred_element_type=jnp.float32)

def reference(ensemble_height_winds, obs_count, obs_cell, obs_value, obs_rinv):
    propagate_ahead = lax.map(explicit_integrator, ensemble_height_winds)
    patch_sequence = propagate_ahead.reshape(ENSEMBLE_SIZE, 3, PATCH_DOWN, PATCH_EDGE_LEN, PATCH_ACROSS, PATCH_EDGE_LEN).transpose(2, 4, 0, 1, 3, 5).reshape(PATCH_DOWN * PATCH_ACROSS, ENSEMBLE_SIZE, 3, PATCH_POINTS)
    means, devs = lax.map(centre_region, patch_sequence)

    def one_block(inputs):
        deviation, cell_ids, number, measured, precision = inputs
        heights = deviation[:, :PATCH_POINTS].astype(jnp.float32)
        return make_block(jnp.take(heights, cell_ids, axis=1), number, measured, precision)
    blocks = lax.map(one_block, (devs, obs_cell.reshape(PATCH_DOWN * PATCH_ACROSS, PMAX), obs_count.reshape(PATCH_DOWN * PATCH_ACROSS), obs_value.reshape(PATCH_DOWN * PATCH_ACROSS, PMAX), obs_rinv.reshape(PATCH_DOWN * PATCH_ACROSS, PMAX)))
    blocks = blocks.reshape(PATCH_DOWN, PATCH_ACROSS, PMAX + 1, ENSEMBLE_SIZE)
    padded_blocks = jnp.pad(blocks, ((1, 1), (1, 1), (0, 0), (0, 0)))
    zero_index = jnp.zeros((), jnp.int32)

    def one_region(region_index):
        row_at = (region_index // PATCH_ACROSS).astype(jnp.int32)
        col_at = (region_index % PATCH_ACROSS).astype(jnp.int32)
        neighbourhood = lax.dynamic_slice(padded_blocks, (row_at, col_at, zero_index, zero_index), (3, 3, PMAX + 1, ENSEMBLE_SIZE))
        ens_mean = lax.dynamic_index_in_dim(means, region_index, 0, keepdims=False)
        deviation = lax.dynamic_index_in_dim(devs, region_index, 0, keepdims=False)
        return analyse(neighbourhood, ens_mean, deviation)
    result = lax.map(one_region, jnp.arange(PATCH_DOWN * PATCH_ACROSS, dtype=jnp.int32))
    return result.reshape(PATCH_DOWN, PATCH_ACROSS, ENSEMBLE_SIZE, 3, PATCH_POINTS)
```

```python
import functools
import math

import jax
import jax.numpy as jnp
from jax import lax
from jax.experimental import pallas as pl
from jax.experimental.pallas import tpu as pltpu
from jax.sharding import PartitionSpec as P

PATCH_EDGE_LEN = 16
NS_ITERS = 5
GRAVITY = 1.0
DEPTH = 1.0
CORIOLIS = 0.25
TIME_STEP = 0.5
LOCALITY = (0.35, 0.6, 1.0)
NEWTON_SCALE = 16.0
HALO = 3
LANES = 128
MESH = pl.DeviceIdType.MESH
OFFSETS = [(p, q) for p in (-1, 0, 1) for q in (-1, 0, 1) if (p, q) != (0, 0)]


def split_rows(row):
    first = row.astype(jnp.bfloat16).astype(jnp.float32)
    second = (row - first).astype(jnp.bfloat16).astype(jnp.float32)
    third = row - first - second
    at = lax.broadcasted_iota(jnp.int32, (16, row.shape[1]), 0)
    rows = jnp.where(at == 0, first, jnp.where(at == 1, second, jnp.where(at == 2, third, 0.0)))
    return rows.astype(jnp.bfloat16)


def dot_nt(a, b):
    return lax.dot_general(a, b, (((1,), (1,)), ((), ())), preferred_element_type=jnp.float32)


def dot_nn(a, b):
    return jnp.dot(a, b, preferred_element_type=jnp.float32)


def step_row(src, row, group, cols):
    size = cols.shape[1]

    def at(field, i):
        return src[field, i, group, :]

    def dx(a):
        right = jnp.where(cols == size - 1, 0.0, pltpu.roll(a, size - 1, 1))
        left = jnp.where(cols == 0, 0.0, pltpu.roll(a, 1, 1))
        return right - left

    h, u, v = at(0, row), at(1, row), at(2, row)
    hm, um, vm = at(0, row - 1), at(1, row - 1), at(2, row - 1)
    hp, up, vp = at(0, row + 1), at(1, row + 1), at(2, row + 1)
    half = 0.5 * TIME_STEP
    turn = CORIOLIS * TIME_STEP
    new_h = h - half * (dx((DEPTH + h) * u) + ((DEPTH + hp) * vp - (DEPTH + hm) * vm))
    new_u = u - half * (u * dx(u) + v * (up - um) + GRAVITY * dx(h)) + turn * v
    new_v = v - half * (u * dx(v) + v * (vp - vm) + GRAVITY * (hp - hm)) - turn * u
    return new_h, new_u, new_v


def kernel(n_mem, n_lat, x_hbm, cnt, cell, val, rinv, out, xs, q, s1, s2, fin, sb, x, dev, bar, nby, nbv,
           yb, zb, mb, load_sem, halo_send, halo_recv, a2a_send, a2a_recv, nb_send, nb_recv):
    me, lat = lax.axis_index("mem"), lax.axis_index("lat")
    _, rows_ext, members, width = q.shape
    lines = rows_ext - 2 * HALO
    ensemble = x.shape[1]
    group_size = min(16, members)
    groups = [pl.ds(g * group_size, group_size) for g in range(members // group_size)]

    barrier = pltpu.get_barrier_semaphore()

    loads = [
        pltpu.make_async_copy(x_hbm.at[:, pl.ds(i * LANES, LANES)], xs.at[i], load_sem.at[i])
        for i in range(width // LANES)
    ]
    for load in loads:
        load.start()

    def greet(k, _):
        pl.semaphore_signal(barrier, inc=1, device_id=(lax.rem(me + k, n_mem), lat), device_id_type=MESH)
        return 0

    lax.fori_loop(1, n_mem, greet, 0)
    beside = [(p, q_) for p in (-1, 1) for q_ in (-1, 0, 1)]
    for p, q_ in beside:
        pl.semaphore_signal(
            barrier, inc=1,
            device_id=(lax.rem(me + q_ + n_mem, n_mem), lax.rem(lat + p + n_lat, n_lat)),
            device_id_type=MESH,
        )
    for load in loads:
        load.wait()
    stride = 3 * lines
    for i in range(width // LANES):
        for f in range(3):
            for r in range(lines):
                q[f, HALO + r, :, i * LANES:(i + 1) * LANES] = xs[i, pl.ds(f * lines + r, members, stride=stride), :]
    pl.semaphore_wait(barrier, n_mem - 1 + len(beside))

    above = (me, lax.rem(lat + n_lat - 1, n_lat))
    below = (me, lax.rem(lat + 1, n_lat))
    halos = [
        pltpu.make_async_remote_copy(
            q.at[:, pl.ds(HALO, HALO)], q.at[:, pl.ds(HALO + lines, HALO)],
            halo_send.at[0], halo_recv.at[0], device_id=above, device_id_type=MESH),
        pltpu.make_async_remote_copy(
            q.at[:, pl.ds(lines, HALO)], q.at[:, pl.ds(0, HALO)],
            halo_send.at[1], halo_recv.at[1], device_id=below, device_id_type=MESH),
    ]
    for halo in halos:
        halo.start()
    for halo in halos:
        halo.wait()

    top = jnp.where(lat > 0, 1.0, 0.0)
    bottom = jnp.where(lat < n_lat - 1, 1.0, 0.0)
    for f in range(3):
        for r in range(HALO):
            q[f, r] = q[f, r] * top
            q[f, HALO + lines + r] = q[f, HALO + lines + r] * bottom

    cols = lax.broadcasted_iota(jnp.int32, (group_size, width), 1)

    def keep(i):
        return jnp.where(i < HALO, top, jnp.where(i >= HALO + lines, bottom, 1.0))

    def first(i, _):
        for group in groups:
            for f, new in enumerate(step_row(q, i, group, cols)):
                s1[f, i, group, :] = new * keep(i)
        return 0

    def second(i, _):
        for group in groups:
            for f, new in enumerate(step_row(s1, i, group, cols)):
                s2[f, i, group, :] = (0.75 * q[f, i, group, :] + 0.25 * new) * keep(i)
        return 0

    def third(i, _):
        for group in groups:
            for f, new in enumerate(step_row(s2, i, group, cols)):
                fin[f, i - HALO, group, :] = q[f, i, group, :] * (1.0 / 3.0) + (2.0 / 3.0) * new
        return 0

    lax.fori_loop(1, rows_ext - 1, first, 0)
    lax.fori_loop(2, rows_ext - 2, second, 0)
    lax.fori_loop(3, rows_ext - 3, third, 0)

    per = LANES // PATCH_EDGE_LEN
    lane_group = lax.broadcasted_iota(jnp.int32, (group_size, LANES), 1) // PATCH_EDGE_LEN
    mine = pl.ds(pl.multiple_of(me * members, members), members)

    def part(f, k):
        target = lax.rem(me + k, n_mem)
        return pltpu.make_async_remote_copy(
            sb.at[target, f], x.at[f, mine], a2a_send.at[f, k], a2a_recv.at[f, k],
            device_id=(target, lat), device_id_type=MESH)

    for f in range(3):
        def regroup(hb, _, f=f):
            lanes = pl.ds(pl.multiple_of(hb * LANES, LANES), LANES)
            for hr in range(lines // per):
                for group in groups:
                    v = [fin[f, hr * per + i, group, lanes] for i in range(per)]
                    k = per // 2
                    while k:
                        high = (lane_group & k) > 0
                        for i in range(per):
                            if not i & k:
                                lo, hi = v[i], v[i + k]
                                v[i] = jnp.where(high, pltpu.roll(hi, PATCH_EDGE_LEN * k, 1), lo)
                                v[i + k] = jnp.where(high, hi, pltpu.roll(lo, LANES - PATCH_EDGE_LEN * k, 1))
                        k //= 2
                    for j in range(per):
                        sb[hb * per + j, f, group, hr * LANES:(hr + 1) * LANES] = v[j].astype(sb.dtype)
            return 0

        lax.fori_loop(0, width // LANES, regroup, 0)

        def send(k, _, f=f):
            part(f, k).start()
            return 0

        lax.fori_loop(1, n_mem, send, 0)
        x[f, mine, :] = sb[me, f]

    def arrive(f):
        def wait(k, _):
            part(f, k).wait()
            return 0

        lax.fori_loop(1, n_mem, wait, 0)

    def centre(f):
        total = x[f].astype(jnp.float32)
        mean = jnp.sum(total, axis=0, keepdims=True) * (1.0 / ensemble)
        bar[f] = jnp.broadcast_to(mean, bar.shape[1:])
        dev[f] = (total - mean).astype(jnp.bfloat16)

    arrive(0)
    centre(0)

    slots = cell.shape[2]
    cells = lax.broadcasted_iota(jnp.int32, (x.shape[2], slots), 0)
    one_hot = jnp.where(cells == cell[0, pl.ds(me, 1), :], 1.0, 0.0).astype(jnp.bfloat16)
    hx = dot_nn(dev[0], one_hot)
    ybar = jnp.sum(hx, axis=0, keepdims=True) * (1.0 / ensemble)
    slot = lax.broadcasted_iota(jnp.int32, (1, slots), 1)
    weight = jnp.where(slot < cnt[0, me], jnp.sqrt(rinv[0, pl.ds(me, 1), :]), 0.0)
    nby[4] = (weight * (hx - ybar) / math.sqrt(ensemble - 1)).astype(jnp.bfloat16)
    misfit = weight * (val[0, pl.ds(me, 1), :] - ybar)
    summary = jnp.sum(dot_nt(split_rows(misfit), nby[4]), axis=0, keepdims=True)
    nbv[4] = jnp.broadcast_to(summary, nbv.shape[1:]).astype(jnp.bfloat16)

    def inside(p, q_):
        return (lat + p >= 0) & (lat + p < n_lat) & (me + q_ >= 0) & (me + q_ < n_mem)

    def block(p, q_):
        slot_there = (1 - p) * 3 + (1 - q_)
        return [
            pltpu.make_async_remote_copy(
                src.at[4], src.at[slot_there], nb_send.at[i, slot_there], nb_recv.at[i, slot_there],
                device_id=(me + q_, lat + p), device_id_type=MESH)
            for i, src in enumerate((nby, nbv))
        ]

    for p, q_ in OFFSETS:
        @pl.when(inside(p, q_))
        def _(p=p, q_=q_):
            for copy in block(p, q_):
                copy.start()

    for p, q_ in OFFSETS:
        here = (1 + p) * 3 + 1 + q_

        @pl.when(inside(p, q_))
        def _(p=p, q_=q_, here=here):
            for copy in block(p, q_):
                copy.wait_send()
            for i, dst in enumerate((nby, nbv)):
                pltpu.make_async_remote_copy(
                    dst.at[4], dst.at[here], nb_send.at[i, here], nb_recv.at[i, here],
                    device_id=(me + q_, lat + p), device_id_type=MESH).wait_recv()

        @pl.when(jnp.logical_not(inside(p, q_)))
        def _(here=here):
            nby[here] = jnp.zeros(nby.shape[1:], jnp.bfloat16)
            nbv[here] = jnp.zeros(nbv.shape[1:], jnp.bfloat16)

    edges, corners = (1, 3, 5, 7), (0, 2, 6, 8)
    drive = nbv[4, 0:1, :].astype(jnp.float32)
    for i in edges:
        drive = drive + LOCALITY[1] * nbv[i, 0:1, :].astype(jnp.float32)
    for i in corners:
        drive = drive + LOCALITY[0] * nbv[i, 0:1, :].astype(jnp.float32)

    tile = ensemble // 2

    def eye(r):
        rows = lax.broadcasted_iota(jnp.int32, (tile, ensemble), 0) + r * tile
        return jnp.where(rows == lax.broadcasted_iota(jnp.int32, (tile, ensemble), 1), 1.0, 0.0)

    halves = [slice(r * tile, (r + 1) * tile) for r in range(2)]
    for r, at in enumerate(halves):
        gram = dot_nt(nby[4, at], nby[4])
        for w, which in ((LOCALITY[1], edges), (LOCALITY[0], corners)):
            left = jnp.concatenate([nby[i, at] for i in which], axis=1)
            gram = gram + w * dot_nt(left, jnp.concatenate([nby[i] for i in which], axis=1))
        root = ((eye(r) + gram) * (1.0 / NEWTON_SCALE)).astype(jnp.bfloat16)
        yb[0, at] = root
        mb[at] = (1.5 * eye(r) - 0.5 * root.astype(jnp.float32)).astype(jnp.bfloat16)

    for sweep in range(NS_ITERS):
        now, then = sweep % 2, (sweep + 1) % 2
        if sweep > 0:
            for r, at in enumerate(halves):
                product = dot_nn(yb[now, at], zb[now])
                mb[at] = (1.5 * eye(r) - 0.5 * product).astype(jnp.bfloat16)
        for at in halves:
            if sweep + 1 < NS_ITERS:
                yb[then, at] = dot_nn(mb[at], yb[now]).astype(jnp.bfloat16)
            if sweep > 0:
                zb[then, at] = dot_nn(zb[now, at], mb[...]).astype(jnp.bfloat16)
            else:
                zb[then, at] = mb[at]
    last = NS_ITERS % 2
    inner = jnp.sum(dot_nn(split_rows(drive), zb[last]), axis=0, keepdims=True)
    weights = jnp.sum(dot_nn(split_rows(inner), zb[last]), axis=0, keepdims=True) * (1.0 / NEWTON_SCALE)
    shift = weights * (1.0 / math.sqrt(ensemble - 1))
    mb[...] = (shift + zb[last].astype(jnp.float32) * (1.0 / math.sqrt(NEWTON_SCALE))).astype(jnp.bfloat16)

    for f in range(3):
        if f > 0:
            arrive(f)
            centre(f)
        out[f] = bar[f, 0:1, :] + dot_nn(mb[...], dev[f])


def per_device(n_mem, n_lat, ensemble_height_winds, obs_count, obs_cell, obs_value, obs_rinv):
    members, fields, lines, width = ensemble_height_winds.shape
    ensemble = members * n_mem
    cells = PATCH_EDGE_LEN * PATCH_EDGE_LEN
    slots = obs_cell.shape[2]
    link = jnp.bfloat16 if members % 16 == 0 else jnp.float32
    rows_ext = lines + 2 * HALO
    vmem = pl.BlockSpec(memory_space=pltpu.VMEM)
    dma = pltpu.SemaphoreType.DMA
    out = pl.pallas_call(
        functools.partial(kernel, n_mem, n_lat),
        out_shape=jax.ShapeDtypeStruct((fields, ensemble, cells), jnp.float32),
        in_specs=[
            pl.BlockSpec(memory_space=pl.ANY),
            pl.BlockSpec(memory_space=pltpu.SMEM),
            vmem, vmem, vmem,
        ],
        out_specs=vmem,
        scratch_shapes=[
            pltpu.VMEM((width // LANES, members * fields * lines, LANES), jnp.float32),
            pltpu.VMEM((fields, rows_ext, members, width), jnp.float32),
            pltpu.VMEM((fields, rows_ext, members, width), jnp.float32),
            pltpu.VMEM((fields, rows_ext, members, width), jnp.float32),
            pltpu.VMEM((fields, lines, members, width), jnp.float32),
            pltpu.VMEM((n_mem, fields, members, cells), link),
            pltpu.VMEM((fields, ensemble, cells), link),
            pltpu.VMEM((fields, ensemble, cells), jnp.bfloat16),
            pltpu.VMEM((fields, 8, cells), jnp.float32),
            pltpu.VMEM((9, ensemble, slots), jnp.bfloat16),
            pltpu.VMEM((9, 16, ensemble), jnp.bfloat16),
            pltpu.VMEM((2, ensemble, ensemble), jnp.bfloat16),
            pltpu.VMEM((2, ensemble, ensemble), jnp.bfloat16),
            pltpu.VMEM((ensemble, ensemble), jnp.bfloat16),
            dma((width // LANES,)),
            dma((2,)), dma((2,)),
            dma((fields, n_mem)), dma((fields, n_mem)),
            dma((2, 9)), dma((2, 9)),
        ],
        compiler_params=pltpu.CompilerParams(
            collective_id=0, has_side_effects=True, vmem_limit_bytes=48 * 1024 * 1024
        ),
    )(
        ensemble_height_winds.reshape(members * fields * lines, width),
        obs_count, obs_cell, obs_value, obs_rinv,
    )
    return out.transpose(1, 0, 2)[None, None]


def solution(mesh):
    in_specs = (
        P("mem", None, "lat", None),
        P("lat", None),
        P("lat", None, None),
        P("lat", None, None),
        P("lat", None, None),
    )
    out_specs = P("lat", "mem", None, None, None)
    return jax.shard_map(
        functools.partial(per_device, mesh.shape["mem"], mesh.shape["lat"]),
        mesh=mesh, in_specs=in_specs, out_specs=out_specs, check_vma=False
    )
```

```python
import functools
import math

import jax
import jax.numpy as jnp
from jax import lax
from jax.experimental import pallas as pl
from jax.experimental.pallas import tpu as pltpu
from jax.sharding import PartitionSpec as P

PATCH_EDGE_LEN = 16
NS_ITERS = 5
GRAVITY = 1.0
DEPTH = 1.0
CORIOLIS = 0.25
TIME_STEP = 0.5
LOCALITY = (0.35, 0.6, 1.0)
NEWTON_SCALE = 16.0
HALO = 3
LANES = 128
MESH = pl.DeviceIdType.MESH
OFFSETS = [(p, q) for p in (-1, 0, 1) for q in (-1, 0, 1) if (p, q) != (0, 0)]


def split_rows(row):
    first = row.astype(jnp.bfloat16).astype(jnp.float32)
    second = (row - first).astype(jnp.bfloat16).astype(jnp.float32)
    third = row - first - second
    at = lax.broadcasted_iota(jnp.int32, (16, row.shape[1]), 0)
    rows = jnp.where(at == 0, first, jnp.where(at == 1, second, jnp.where(at == 2, third, 0.0)))
    return rows.astype(jnp.bfloat16)


def dot_nt(a, b):
    return lax.dot_general(a, b, (((1,), (1,)), ((), ())), preferred_element_type=jnp.float32)


def dot_nn(a, b):
    return jnp.dot(a, b, preferred_element_type=jnp.float32)


def step_row(src, row, group, cols):
    size = cols.shape[1]

    def at(field, i):
        return src[field, i, group, :]

    def dx(a):
        right = jnp.where(cols == size - 1, 0.0, pltpu.roll(a, size - 1, 1))
        left = jnp.where(cols == 0, 0.0, pltpu.roll(a, 1, 1))
        return right - left

    h, u, v = at(0, row), at(1, row), at(2, row)
    hm, um, vm = at(0, row - 1), at(1, row - 1), at(2, row - 1)
    hp, up, vp = at(0, row + 1), at(1, row + 1), at(2, row + 1)
    half = 0.5 * TIME_STEP
    turn = CORIOLIS * TIME_STEP
    new_h = h - half * (dx((DEPTH + h) * u) + ((DEPTH + hp) * vp - (DEPTH + hm) * vm))
    new_u = u - half * (u * dx(u) + v * (up - um) + GRAVITY * dx(h)) + turn * v
    new_v = v - half * (u * dx(v) + v * (vp - vm) + GRAVITY * (hp - hm)) - turn * u
    return new_h, new_u, new_v


def kernel(n_mem, n_lat, x_hbm, cnt_hbm, cell_hbm, val_hbm, rinv_hbm, mb_out, dev_out, bar_out, cnt, cell, val, rinv, xs, q, s1, s2, fin, sb, x, dev, bar, nby, nbv,
           yb, zb, mb, out_sem, obs_sem, load_sem, halo_send, halo_recv, a2a_send, a2a_recv, nb_send, nb_recv):
    me, lat = lax.axis_index("mem"), lax.axis_index("lat")
    _, rows_ext, members, width = q.shape
    lines = rows_ext - 2 * HALO
    ensemble = x.shape[1]
    group_size = min(16, members)
    groups = [pl.ds(g * group_size, group_size) for g in range(members // group_size)]

    barrier = pltpu.get_barrier_semaphore()

    loads = [
        pltpu.make_async_copy(x_hbm.at[:, pl.ds(i * LANES, LANES)], xs.at[i], load_sem.at[i])
        for i in range(width // LANES)
    ]
    for load in loads:
        load.start()
    obs_loads = [
        pltpu.make_async_copy(src, dst, obs_sem.at[i])
        for i, (src, dst) in enumerate(((cnt_hbm, cnt), (cell_hbm, cell), (val_hbm, val), (rinv_hbm, rinv)))
    ]
    for load in obs_loads:
        load.start()

    def greet(k, _):
        pl.semaphore_signal(barrier, inc=1, device_id=(lax.rem(me + k, n_mem), lat), device_id_type=MESH)
        return 0

    lax.fori_loop(1, n_mem, greet, 0)
    beside = [(p, q_) for p in (-1, 1) for q_ in (-1, 0, 1)]
    for p, q_ in beside:
        pl.semaphore_signal(
            barrier, inc=1,
            device_id=(lax.rem(me + q_ + n_mem, n_mem), lax.rem(lat + p + n_lat, n_lat)),
            device_id_type=MESH,
        )
    for load in loads:
        load.wait()
    stride = 3 * lines
    for i in range(width // LANES):
        for f in range(3):
            for r in range(lines):
                q[f, HALO + r, :, i * LANES:(i + 1) * LANES] = xs[i, pl.ds(f * lines + r, members, stride=stride), :]
    pl.semaphore_wait(barrier, n_mem - 1 + len(beside))

    above = (me, lax.rem(lat + n_lat - 1, n_lat))
    below = (me, lax.rem(lat + 1, n_lat))
    halos = [
        pltpu.make_async_remote_copy(
            q.at[:, pl.ds(HALO, HALO)], q.at[:, pl.ds(HALO + lines, HALO)],
            halo_send.at[0], halo_recv.at[0], device_id=above, device_id_type=MESH),
        pltpu.make_async_remote_copy(
            q.at[:, pl.ds(lines, HALO)], q.at[:, pl.ds(0, HALO)],
            halo_send.at[1], halo_recv.at[1], device_id=below, device_id_type=MESH),
    ]
    for halo in halos:
        halo.start()
    top = jnp.where(lat > 0, 1.0, 0.0)
    bottom = jnp.where(lat < n_lat - 1, 1.0, 0.0)
    cols = lax.broadcasted_iota(jnp.int32, (group_size, width), 1)

    def keep(i):
        return jnp.where(i < HALO, top, jnp.where(i >= HALO + lines, bottom, 1.0))

    def first(i, group):
        for f, new in enumerate(step_row(q, i, group, cols)):
            s1[f, i, group, :] = new * keep(i)

    def second(i, group):
        for f, new in enumerate(step_row(s1, i, group, cols)):
            s2[f, i, group, :] = (0.75 * q[f, i, group, :] + 0.25 * new) * keep(i)

    def third(i, group):
        for f, new in enumerate(step_row(s2, i, group, cols)):
            fin[f, i - HALO, group, :] = q[f, i, group, :] * (1.0 / 3.0) + (2.0 / 3.0) * new

    def over_rows(stage, low, high, group):
        def pair(i, _):
            stage(low + 2 * i, group)
            stage(low + 2 * i + 1, group)
            return 0

        lax.fori_loop(0, (high - low) // 2, pair, 0)

    per = LANES // PATCH_EDGE_LEN
    lane_group = lax.broadcasted_iota(jnp.int32, (group_size, LANES), 1) // PATCH_EDGE_LEN

    def part(f, g, k):
        target = lax.rem(me + k, n_mem)
        mine = pl.ds(pl.multiple_of(me * members + g * group_size, group_size), group_size)
        return pltpu.make_async_remote_copy(
            sb.at[target, f, groups[g]], x.at[f, mine], a2a_send.at[f, g, k], a2a_recv.at[f, g, k],
            device_id=(target, lat), device_id_type=MESH)

    def regroup(f, g):
        group = groups[g]

        def body(hb, _):
            lanes = pl.ds(pl.multiple_of(hb * LANES, LANES), LANES)
            for hr in range(lines // per):
                v = [fin[f, hr * per + i, group, lanes] for i in range(per)]
                k = per // 2
                while k:
                    high = (lane_group & k) > 0
                    for i in range(per):
                        if not i & k:
                            lo, hi = v[i], v[i + k]
                            v[i] = jnp.where(high, pltpu.roll(hi, PATCH_EDGE_LEN * k, 1), lo)
                            v[i + k] = jnp.where(high, hi, pltpu.roll(lo, LANES - PATCH_EDGE_LEN * k, 1))
                    k //= 2
                for j in range(per):
                    sb[hb * per + j, f, group, hr * LANES:(hr + 1) * LANES] = v[j].astype(sb.dtype)
            return 0

        lax.fori_loop(0, width // LANES, body, 0)

    def send(f, g):
        def one(k, _):
            part(f, g, k).start()
            return 0

        lax.fori_loop(1, n_mem, one, 0)
        x[f, pl.ds(pl.multiple_of(me * members + g * group_size, group_size), group_size), :] = sb[me, f, groups[g]]

    def arrive(f):
        def wait(k, _):
            for g in range(len(groups)):
                part(f, g, k).wait()
            return 0

        lax.fori_loop(1, n_mem, wait, 0)

    def centre(f):
        total = x[f].astype(jnp.float32)
        mean = jnp.sum(total, axis=0, keepdims=True) * (1.0 / ensemble)
        bar[f] = jnp.broadcast_to(mean, bar.shape[1:])
        dev[f] = (total - mean).astype(jnp.bfloat16)

    later = []
    for g, group in enumerate(groups):
        over_rows(first, HALO + 1, HALO + lines - 1, group)
        if g == 0:
            for halo in halos:
                halo.wait()
            for f in range(3):
                for r in range(HALO):
                    q[f, r] = q[f, r] * top
                    q[f, HALO + lines + r] = q[f, HALO + lines + r] * bottom

        def edge(j, _, group=group):
            first(j + 1, group)
            first(j + lines + HALO - 1, group)
            return 0

        lax.fori_loop(0, HALO, edge, 0)
        over_rows(second, 2, rows_ext - 2, group)
        over_rows(third, 3, rows_ext - 3, group)
        regroup(0, g)
        send(0, g)
        for f in (1, 2):
            regroup(f, g)
            if f == 1 and g + 1 < len(groups):
                send(f, g)
            else:
                later.append((f, g))
    for load in obs_loads:
        load.wait()

    def leave(f):
        return pltpu.make_async_copy(dev.at[f], dev_out.at[f], out_sem.at[f])

    arrive(0)
    centre(0)
    leave(0).start()

    slots = cell.shape[2]
    cells = lax.broadcasted_iota(jnp.int32, (x.shape[2], slots), 0)
    one_hot = jnp.where(cells == cell[0, pl.ds(me, 1), :], 1.0, 0.0).astype(jnp.bfloat16)
    hx = dot_nn(dev[0], one_hot)
    ybar = jnp.sum(hx, axis=0, keepdims=True) * (1.0 / ensemble)
    slot = lax.broadcasted_iota(jnp.int32, (1, slots), 1)
    count = jnp.sum(
        jnp.where(lax.broadcasted_iota(jnp.int32, cnt.shape, 1) == me, cnt[...], 0), axis=1, keepdims=True)
    weight = jnp.where(slot < count, jnp.sqrt(rinv[0, pl.ds(me, 1), :]), 0.0)
    nby[4] = (weight * (hx - ybar) / math.sqrt(ensemble - 1)).astype(jnp.bfloat16)
    misfit = weight * (val[0, pl.ds(me, 1), :] - ybar)
    summary = jnp.sum(dot_nt(split_rows(misfit), nby[4]), axis=0, keepdims=True)
    nbv[4] = jnp.broadcast_to(summary, nbv.shape[1:]).astype(jnp.bfloat16)

    def inside(p, q_):
        return (lat + p >= 0) & (lat + p < n_lat) & (me + q_ >= 0) & (me + q_ < n_mem)

    def block(p, q_):
        slot_there = (1 - p) * 3 + (1 - q_)
        return [
            pltpu.make_async_remote_copy(
                src.at[4], src.at[slot_there], nb_send.at[i, slot_there], nb_recv.at[i, slot_there],
                device_id=(me + q_, lat + p), device_id_type=MESH)
            for i, src in enumerate((nby, nbv))
        ]

    for p, q_ in OFFSETS:
        @pl.when(inside(p, q_))
        def _(p=p, q_=q_):
            for copy in block(p, q_):
                copy.start()

    for f, g in sorted(later):
        send(f, g)

    for p, q_ in OFFSETS:
        here = (1 + p) * 3 + 1 + q_

        @pl.when(inside(p, q_))
        def _(p=p, q_=q_, here=here):
            for copy in block(p, q_):
                copy.wait_send()
            for i, dst in enumerate((nby, nbv)):
                pltpu.make_async_remote_copy(
                    dst.at[4], dst.at[here], nb_send.at[i, here], nb_recv.at[i, here],
                    device_id=(me + q_, lat + p), device_id_type=MESH).wait_recv()

        @pl.when(jnp.logical_not(inside(p, q_)))
        def _(here=here):
            nby[here] = jnp.zeros(nby.shape[1:], jnp.bfloat16)
            nbv[here] = jnp.zeros(nbv.shape[1:], jnp.bfloat16)

    edges, corners = (1, 3, 5, 7), (0, 2, 6, 8)
    drive = nbv[4, 0:1, :].astype(jnp.float32)
    for i in edges:
        drive = drive + LOCALITY[1] * nbv[i, 0:1, :].astype(jnp.float32)
    for i in corners:
        drive = drive + LOCALITY[0] * nbv[i, 0:1, :].astype(jnp.float32)

    tile = ensemble // 2

    def eye(r):
        rows = lax.broadcasted_iota(jnp.int32, (tile, ensemble), 0) + r * tile
        return jnp.where(rows == lax.broadcasted_iota(jnp.int32, (tile, ensemble), 1), 1.0, 0.0)

    halves = [slice(r * tile, (r + 1) * tile) for r in range(2)]
    for r, at in enumerate(halves):
        gram = dot_nt(nby[4, at], nby[4])
        for w, which in ((LOCALITY[1], edges), (LOCALITY[0], corners)):
            left = jnp.concatenate([nby[i, at] for i in which], axis=1)
            gram = gram + w * dot_nt(left, jnp.concatenate([nby[i] for i in which], axis=1))
        root = ((eye(r) + gram) * (1.0 / NEWTON_SCALE)).astype(jnp.bfloat16)
        yb[0, at] = root
        mb[at] = (1.5 * eye(r) - 0.5 * root.astype(jnp.float32)).astype(jnp.bfloat16)

    for sweep in range(NS_ITERS):
        now, then = sweep % 2, (sweep + 1) % 2
        if sweep > 0:
            for r, at in enumerate(halves):
                product = dot_nn(yb[now, at], zb[now])
                mb[at] = (1.5 * eye(r) - 0.5 * product).astype(jnp.bfloat16)
        for at in halves:
            if sweep + 1 < NS_ITERS:
                yb[then, at] = dot_nn(mb[at], yb[now]).astype(jnp.bfloat16)
            if sweep > 0:
                zb[then, at] = dot_nn(zb[now, at], mb[...]).astype(jnp.bfloat16)
            else:
                zb[then, at] = mb[at]
    last = NS_ITERS % 2
    inner = jnp.sum(dot_nn(split_rows(drive), zb[last]), axis=0, keepdims=True)
    weights = jnp.sum(dot_nn(split_rows(inner), zb[last]), axis=0, keepdims=True) * (1.0 / NEWTON_SCALE)
    shift = weights * (1.0 / math.sqrt(ensemble - 1))
    mb[...] = (shift + zb[last].astype(jnp.float32) * (1.0 / math.sqrt(NEWTON_SCALE))).astype(jnp.bfloat16)

    transform_out = pltpu.make_async_copy(mb, mb_out, out_sem.at[3])
    transform_out.start()
    for f in (1, 2):
        arrive(f)
        centre(f)
        leave(f).start()
    means_out = pltpu.make_async_copy(bar, bar_out, out_sem.at[4])
    means_out.start()
    for f in range(3):
        leave(f).wait()
    transform_out.wait()
    means_out.wait()


def apply_transform(mb, dev, bar, out):
    out[0] = bar[0, 0:1, :] + dot_nn(mb[...], dev[0])


def per_device(n_mem, n_lat, ensemble_height_winds, obs_count, obs_cell, obs_value, obs_rinv):
    members, fields, lines, width = ensemble_height_winds.shape
    ensemble = members * n_mem
    cells = PATCH_EDGE_LEN * PATCH_EDGE_LEN
    slots = obs_cell.shape[2]
    link = jnp.bfloat16 if members % 16 == 0 else jnp.float32
    rows_ext = lines + 2 * HALO
    groups = members // min(16, members)
    dma = pltpu.SemaphoreType.DMA
    transform, deviations, means = pl.pallas_call(
        functools.partial(kernel, n_mem, n_lat),
        out_shape=(
            jax.ShapeDtypeStruct((ensemble, ensemble), jnp.bfloat16),
            jax.ShapeDtypeStruct((fields, ensemble, cells), jnp.bfloat16),
            jax.ShapeDtypeStruct((fields, 8, cells), jnp.float32),
        ),
        in_specs=[pl.BlockSpec(memory_space=pltpu.HBM)] * 5,
        out_specs=[pl.BlockSpec(memory_space=pltpu.HBM)] * 3,
        scratch_shapes=[
            *(pltpu.VMEM(a.shape, a.dtype) for a in (obs_count, obs_cell, obs_value, obs_rinv)),
            pltpu.VMEM((width // LANES, members * fields * lines, LANES), jnp.float32),
            pltpu.VMEM((fields, rows_ext, members, width), jnp.float32),
            pltpu.VMEM((fields, rows_ext, members, width), jnp.float32),
            pltpu.VMEM((fields, rows_ext, members, width), jnp.float32),
            pltpu.VMEM((fields, lines, members, width), jnp.float32),
            pltpu.VMEM((n_mem, fields, members, cells), link),
            pltpu.VMEM((fields, ensemble, cells), link),
            pltpu.VMEM((fields, ensemble, cells), jnp.bfloat16),
            pltpu.VMEM((fields, 8, cells), jnp.float32),
            pltpu.VMEM((9, ensemble, slots), jnp.bfloat16),
            pltpu.VMEM((9, 16, ensemble), jnp.bfloat16),
            pltpu.VMEM((2, ensemble, ensemble), jnp.bfloat16),
            pltpu.VMEM((2, ensemble, ensemble), jnp.bfloat16),
            pltpu.VMEM((ensemble, ensemble), jnp.bfloat16),
            dma((5,)),
            dma((4,)),
            dma((width // LANES,)),
            dma((2,)), dma((2,)),
            dma((fields, groups, n_mem)), dma((fields, groups, n_mem)),
            dma((2, 9)), dma((2, 9)),
        ],
        compiler_params=pltpu.CompilerParams(
            collective_id=0, has_side_effects=True, vmem_limit_bytes=62 * 1024 * 1024
        ),
    )(
        ensemble_height_winds.reshape(members * fields * lines, width),
        obs_count, obs_cell, obs_value, obs_rinv,
    )
    out = pl.pallas_call(
        apply_transform,
        grid=(fields,),
        out_shape=jax.ShapeDtypeStruct((fields, ensemble, cells), jnp.float32),
        in_specs=[
            pl.BlockSpec((ensemble, ensemble), lambda f: (0, 0)),
            pl.BlockSpec((1, ensemble, cells), lambda f: (f, 0, 0)),
            pl.BlockSpec((1, 8, cells), lambda f: (f, 0, 0)),
        ],
        out_specs=pl.BlockSpec((1, ensemble, cells), lambda f: (f, 0, 0)),
    )(transform, deviations, means)
    return out.transpose(1, 0, 2)[None, None]


def solution(mesh):
    in_specs = (
        P("mem", None, "lat", None),
        P("lat", None),
        P("lat", None, None),
        P("lat", None, None),
        P("lat", None, None),
    )
    out_specs = P("lat", "mem", None, None, None)
    return jax.shard_map(
        functools.partial(per_device, mesh.shape["mem"], mesh.shape["lat"]),
        mesh=mesh, in_specs=in_specs, out_specs=out_specs, check_vma=False
    )
```

```python
import functools
import math

import jax
import jax.numpy as jnp
from jax import lax
from jax.experimental import pallas as pl
from jax.experimental.pallas import tpu as pltpu
from jax.sharding import PartitionSpec as P

PATCH_EDGE_LEN = 16
NS_ITERS = 5
GRAVITY = 1.0
DEPTH = 1.0
CORIOLIS = 0.25
TIME_STEP = 0.5
LOCALITY = (0.35, 0.6, 1.0)
NEWTON_SCALE = 16.0
HALO = 3
LANES = 128
MESH = pl.DeviceIdType.MESH


def split_rows(row):
    first = row.astype(jnp.bfloat16).astype(jnp.float32)
    second = (row - first).astype(jnp.bfloat16).astype(jnp.float32)
    third = row - first - second
    at = lax.broadcasted_iota(jnp.int32, (16, row.shape[1]), 0)
    rows = jnp.where(at == 0, first, jnp.where(at == 1, second, jnp.where(at == 2, third, 0.0)))
    return rows.astype(jnp.bfloat16)


def dot_nt(a, b):
    return lax.dot_general(a, b, (((1,), (1,)), ((), ())), preferred_element_type=jnp.float32)


def dot_nn(a, b):
    return jnp.dot(a, b, preferred_element_type=jnp.float32)


def step_row(src, row, group, cols):
    size = cols.shape[1]

    def at(field, i):
        return src[field, i, group, :]

    def dx(a):
        right = jnp.where(cols == size - 1, 0.0, pltpu.roll(a, size - 1, 1))
        left = jnp.where(cols == 0, 0.0, pltpu.roll(a, 1, 1))
        return right - left

    h, u, v = at(0, row), at(1, row), at(2, row)
    hm, um, vm = at(0, row - 1), at(1, row - 1), at(2, row - 1)
    hp, up, vp = at(0, row + 1), at(1, row + 1), at(2, row + 1)
    half = 0.5 * TIME_STEP
    turn = CORIOLIS * TIME_STEP
    new_h = h - half * (dx((DEPTH + h) * u) + ((DEPTH + hp) * vp - (DEPTH + hm) * vm))
    new_u = u - half * (u * dx(u) + v * (up - um) + GRAVITY * dx(h)) + turn * v
    new_v = v - half * (u * dx(v) + v * (vp - vm) + GRAVITY * (hp - hm)) - turn * u
    return new_h, new_u, new_v


def kernel(n_mem, n_lat, x_hbm, cnt_hbm, cell_hbm, val_hbm, rinv_hbm, mb_out, dev_out, bar_out, cnt, cell, val, rinv, xs, q, s1, s2, fin, sb, x, dev, bar, nby, nbv,
           yb, zb, mb, out_sem, obs_sem, load_sem, halo_send, halo_recv, a2a_send, a2a_recv, nb_send, nb_recv):
    me, lat = lax.axis_index("mem"), lax.axis_index("lat")
    _, rows_ext, members, width = q.shape
    lines = rows_ext - 2 * HALO
    ensemble = x.shape[1]
    group_size = min(16, members)
    groups = [pl.ds(g * group_size, group_size) for g in range(members // group_size)]

    barrier = pltpu.get_barrier_semaphore()

    loads = [
        pltpu.make_async_copy(x_hbm.at[:, pl.ds(i * LANES, LANES)], xs.at[i], load_sem.at[i])
        for i in range(width // LANES)
    ]
    for load in loads:
        load.start()
    obs_loads = [
        pltpu.make_async_copy(src, dst, obs_sem.at[i])
        for i, (src, dst) in enumerate(((cnt_hbm, cnt), (cell_hbm, cell), (val_hbm, val), (rinv_hbm, rinv)))
    ]
    for load in obs_loads:
        load.start()

    def greet(k, _):
        pl.semaphore_signal(barrier, inc=1, device_id=(lax.rem(me + k, n_mem), lat), device_id_type=MESH)
        return 0

    lax.fori_loop(1, n_mem, greet, 0)
    beside = [(p, q_) for p in (-1, 1) for q_ in (-1, 0, 1)]
    for p, q_ in beside:
        pl.semaphore_signal(
            barrier, inc=1,
            device_id=(lax.rem(me + q_ + n_mem, n_mem), lax.rem(lat + p + n_lat, n_lat)),
            device_id_type=MESH,
        )
    for load in loads:
        load.wait()
    stride = 3 * lines
    for i in range(width // LANES):
        for f in range(3):
            for r in range(lines):
                q[f, HALO + r, :, i * LANES:(i + 1) * LANES] = xs[i, pl.ds(f * lines + r, members, stride=stride), :]
    pl.semaphore_wait(barrier, n_mem - 1 + len(beside))

    above = (me, lax.rem(lat + n_lat - 1, n_lat))
    below = (me, lax.rem(lat + 1, n_lat))
    halos = [
        pltpu.make_async_remote_copy(
            q.at[:, pl.ds(HALO, HALO)], q.at[:, pl.ds(HALO + lines, HALO)],
            halo_send.at[0], halo_recv.at[0], device_id=above, device_id_type=MESH),
        pltpu.make_async_remote_copy(
            q.at[:, pl.ds(lines, HALO)], q.at[:, pl.ds(0, HALO)],
            halo_send.at[1], halo_recv.at[1], device_id=below, device_id_type=MESH),
    ]
    for halo in halos:
        halo.start()
    top = jnp.where(lat > 0, 1.0, 0.0)
    bottom = jnp.where(lat < n_lat - 1, 1.0, 0.0)
    cols = lax.broadcasted_iota(jnp.int32, (group_size, width), 1)

    def keep(i):
        return jnp.where(i < HALO, top, jnp.where(i >= HALO + lines, bottom, 1.0))

    def first(i, group):
        for f, new in enumerate(step_row(q, i, group, cols)):
            s1[f, i, group, :] = new * keep(i)

    def second(i, group):
        for f, new in enumerate(step_row(s1, i, group, cols)):
            s2[f, i, group, :] = (0.75 * q[f, i, group, :] + 0.25 * new) * keep(i)

    def third(i, group):
        for f, new in enumerate(step_row(s2, i, group, cols)):
            fin[f, i - HALO, group, :] = q[f, i, group, :] * (1.0 / 3.0) + (2.0 / 3.0) * new

    def over_rows(stage, low, high, group):
        def pair(i, _):
            stage(low + 2 * i, group)
            stage(low + 2 * i + 1, group)
            return 0

        lax.fori_loop(0, (high - low) // 2, pair, 0)

    per = LANES // PATCH_EDGE_LEN
    lane_group = lax.broadcasted_iota(jnp.int32, (group_size, LANES), 1) // PATCH_EDGE_LEN

    def part(f, g, k):
        target = lax.rem(me + k, n_mem)
        mine = pl.ds(pl.multiple_of(me * members + g * group_size, group_size), group_size)
        return pltpu.make_async_remote_copy(
            sb.at[target, f, groups[g]], x.at[f, mine], a2a_send.at[f, g, k], a2a_recv.at[f, g, k],
            device_id=(target, lat), device_id_type=MESH)

    def regroup(f, g):
        group = groups[g]

        def body(hb, _):
            lanes = pl.ds(pl.multiple_of(hb * LANES, LANES), LANES)
            for hr in range(lines // per):
                v = [fin[f, hr * per + i, group, lanes] for i in range(per)]
                k = per // 2
                while k:
                    high = (lane_group & k) > 0
                    for i in range(per):
                        if not i & k:
                            lo, hi = v[i], v[i + k]
                            v[i] = jnp.where(high, pltpu.roll(hi, PATCH_EDGE_LEN * k, 1), lo)
                            v[i + k] = jnp.where(high, hi, pltpu.roll(lo, LANES - PATCH_EDGE_LEN * k, 1))
                    k //= 2
                for j in range(per):
                    sb[hb * per + j, f, group, hr * LANES:(hr + 1) * LANES] = v[j].astype(sb.dtype)
            return 0

        lax.fori_loop(0, width // LANES, body, 0)

    def send(f, g):
        def one(k, _):
            part(f, g, k).start()
            return 0

        lax.fori_loop(1, n_mem, one, 0)
        x[f, pl.ds(pl.multiple_of(me * members + g * group_size, group_size), group_size), :] = sb[me, f, groups[g]]

    def arrive(f):
        def wait(k, _):
            for g in range(len(groups)):
                part(f, g, k).wait()
            return 0

        lax.fori_loop(1, n_mem, wait, 0)

    def centre(f):
        total = x[f].astype(jnp.float32)
        mean = jnp.sum(total, axis=0, keepdims=True) * (1.0 / ensemble)
        bar[f] = jnp.broadcast_to(mean, bar.shape[1:])
        dev[f] = (total - mean).astype(jnp.bfloat16)

    later = []
    for g, group in enumerate(groups):
        over_rows(first, HALO + 1, HALO + lines - 1, group)
        if g == 0:
            for halo in halos:
                halo.wait()
            for f in range(3):
                for r in range(HALO):
                    q[f, r] = q[f, r] * top
                    q[f, HALO + lines + r] = q[f, HALO + lines + r] * bottom

        def edge(j, _, group=group):
            first(j + 1, group)
            first(j + lines + HALO - 1, group)
            return 0

        lax.fori_loop(0, HALO, edge, 0)
        over_rows(second, 2, rows_ext - 2, group)
        over_rows(third, 3, rows_ext - 3, group)
        regroup(0, g)
        send(0, g)
        for f in (1, 2):
            regroup(f, g)
            if f == 1 and g + 1 < len(groups):
                send(f, g)
            else:
                later.append((f, g))
    for load in obs_loads:
        load.wait()

    def leave(f):
        return pltpu.make_async_copy(dev.at[f], dev_out.at[f], out_sem.at[f])

    arrive(0)
    centre(0)
    leave(0).start()

    slots = cell.shape[2]
    cells = lax.broadcasted_iota(jnp.int32, (x.shape[2], slots), 0)
    one_hot = jnp.where(cells == cell[0, pl.ds(me, 1), :], 1.0, 0.0).astype(jnp.bfloat16)
    hx = dot_nn(dev[0], one_hot)
    ybar = jnp.sum(hx, axis=0, keepdims=True) * (1.0 / ensemble)
    slot = lax.broadcasted_iota(jnp.int32, (1, slots), 1)
    count = jnp.sum(
        jnp.where(lax.broadcasted_iota(jnp.int32, cnt.shape, 1) == me, cnt[...], 0), axis=1, keepdims=True)
    weight = jnp.where(slot < count, jnp.sqrt(rinv[0, pl.ds(me, 1), :]), 0.0)
    nby[4] = (weight * (hx - ybar) / math.sqrt(ensemble - 1)).astype(jnp.bfloat16)
    misfit = weight * (val[0, pl.ds(me, 1), :] - ybar)
    summary = jnp.sum(dot_nt(split_rows(misfit), nby[4]), axis=0, keepdims=True)
    nbv[4] = jnp.broadcast_to(summary, nbv.shape[1:]).astype(jnp.bfloat16)

    def inside(p, q_):
        return (lat + p >= 0) & (lat + p < n_lat) & (me + q_ >= 0) & (me + q_ < n_mem)

    def block(p, q_, source, slot_there):
        return [
            pltpu.make_async_remote_copy(
                src.at[source], src.at[slot_there], nb_send.at[i, slot_there], nb_recv.at[i, slot_there],
                device_id=(me + q_, lat + p), device_id_type=MESH)
            for i, src in enumerate((nby, nbv))
        ]

    def across(q_):
        return block(0, q_, 4, 4 - q_)

    def along(p, c):
        return block(p, 0, 4 + c, (1 - p) * 3 + 1 + c)

    def clear(here):
        nby[here] = jnp.zeros(nby.shape[1:], jnp.bfloat16)
        nbv[here] = jnp.zeros(nbv.shape[1:], jnp.bfloat16)

    for q_ in (-1, 1):
        @pl.when(inside(0, q_))
        def _(q_=q_):
            for copy in across(q_):
                copy.start()

    for p in (-1, 1):
        @pl.when(inside(p, 0))
        def _(p=p):
            for copy in along(p, 0):
                copy.start()

    for f, g in sorted(later):
        send(f, g)

    for q_ in (-1, 1):
        @pl.when(inside(0, q_))
        def _(q_=q_):
            for copy in across(q_):
                copy.wait_send()
            for copy in block(0, q_, 4, 4 + q_):
                copy.wait_recv()

        @pl.when(jnp.logical_not(inside(0, q_)))
        def _(q_=q_):
            clear(4 + q_)

    for p in (-1, 1):
        @pl.when(inside(p, 0))
        def _(p=p):
            for c in (-1, 1):
                for copy in along(p, c):
                    copy.start()

    for p in (-1, 1):
        @pl.when(inside(p, 0))
        def _(p=p):
            for c in (-1, 0, 1):
                for copy in along(p, c):
                    copy.wait_send()
                for copy in block(p, 0, 4 + c, (1 + p) * 3 + 1 + c):
                    copy.wait_recv()

        @pl.when(jnp.logical_not(inside(p, 0)))
        def _(p=p):
            for c in (-1, 0, 1):
                clear((1 + p) * 3 + 1 + c)

    edges, corners = (1, 3, 5, 7), (0, 2, 6, 8)
    drive = nbv[4, 0:1, :].astype(jnp.float32)
    for i in edges:
        drive = drive + LOCALITY[1] * nbv[i, 0:1, :].astype(jnp.float32)
    for i in corners:
        drive = drive + LOCALITY[0] * nbv[i, 0:1, :].astype(jnp.float32)

    tile = ensemble // 2

    def eye(r):
        rows = lax.broadcasted_iota(jnp.int32, (tile, ensemble), 0) + r * tile
        return jnp.where(rows == lax.broadcasted_iota(jnp.int32, (tile, ensemble), 1), 1.0, 0.0)

    halves = [slice(r * tile, (r + 1) * tile) for r in range(2)]
    for r, at in enumerate(halves):
        gram = dot_nt(nby[4, at], nby[4])
        for w, which in ((LOCALITY[1], edges), (LOCALITY[0], corners)):
            left = jnp.concatenate([nby[i, at] for i in which], axis=1)
            gram = gram + w * dot_nt(left, jnp.concatenate([nby[i] for i in which], axis=1))
        root = ((eye(r) + gram) * (1.0 / NEWTON_SCALE)).astype(jnp.bfloat16)
        yb[0, at] = root
        mb[at] = (1.5 * eye(r) - 0.5 * root.astype(jnp.float32)).astype(jnp.bfloat16)

    for sweep in range(NS_ITERS):
        now, then = sweep % 2, (sweep + 1) % 2
        if sweep > 0:
            for r, at in enumerate(halves):
                product = dot_nn(yb[now, at], zb[now])
                mb[at] = (1.5 * eye(r) - 0.5 * product).astype(jnp.bfloat16)
        for at in halves:
            if sweep + 1 < NS_ITERS:
                yb[then, at] = dot_nn(mb[at], yb[now]).astype(jnp.bfloat16)
            if sweep > 0:
                zb[then, at] = dot_nn(zb[now, at], mb[...]).astype(jnp.bfloat16)
            else:
                zb[then, at] = mb[at]
    last = NS_ITERS % 2
    inner = jnp.sum(dot_nn(split_rows(drive), zb[last]), axis=0, keepdims=True)
    weights = jnp.sum(dot_nn(split_rows(inner), zb[last]), axis=0, keepdims=True) * (1.0 / NEWTON_SCALE)
    shift = weights * (1.0 / math.sqrt(ensemble - 1))
    mb[...] = (shift + zb[last].astype(jnp.float32) * (1.0 / math.sqrt(NEWTON_SCALE))).astype(jnp.bfloat16)

    transform_out = pltpu.make_async_copy(mb, mb_out, out_sem.at[3])
    transform_out.start()
    for f in (1, 2):
        arrive(f)
        centre(f)
        leave(f).start()
    means_out = pltpu.make_async_copy(bar, bar_out, out_sem.at[4])
    means_out.start()
    for f in range(3):
        leave(f).wait()
    transform_out.wait()
    means_out.wait()


def apply_transform(mb, dev, bar, out):
    out[0] = bar[0, 0:1, :] + dot_nn(mb[...], dev[0])


def per_device(n_mem, n_lat, ensemble_height_winds, obs_count, obs_cell, obs_value, obs_rinv):
    members, fields, lines, width = ensemble_height_winds.shape
    ensemble = members * n_mem
    cells = PATCH_EDGE_LEN * PATCH_EDGE_LEN
    slots = obs_cell.shape[2]
    link = jnp.bfloat16 if members % 16 == 0 else jnp.float32
    rows_ext = lines + 2 * HALO
    groups = members // min(16, members)
    dma = pltpu.SemaphoreType.DMA
    transform, deviations, means = pl.pallas_call(
        functools.partial(kernel, n_mem, n_lat),
        out_shape=(
            jax.ShapeDtypeStruct((ensemble, ensemble), jnp.bfloat16),
            jax.ShapeDtypeStruct((fields, ensemble, cells), jnp.bfloat16),
            jax.ShapeDtypeStruct((fields, 8, cells), jnp.float32),
        ),
        in_specs=[pl.BlockSpec(memory_space=pltpu.HBM)] * 5,
        out_specs=[pl.BlockSpec(memory_space=pltpu.HBM)] * 3,
        scratch_shapes=[
            *(pltpu.VMEM(a.shape, a.dtype) for a in (obs_count, obs_cell, obs_value, obs_rinv)),
            pltpu.VMEM((width // LANES, members * fields * lines, LANES), jnp.float32),
            pltpu.VMEM((fields, rows_ext, members, width), jnp.float32),
            pltpu.VMEM((fields, rows_ext, members, width), jnp.float32),
            pltpu.VMEM((fields, rows_ext, members, width), jnp.float32),
            pltpu.VMEM((fields, lines, members, width), jnp.float32),
            pltpu.VMEM((n_mem, fields, members, cells), link),
            pltpu.VMEM((fields, ensemble, cells), link),
            pltpu.VMEM((fields, ensemble, cells), jnp.bfloat16),
            pltpu.VMEM((fields, 8, cells), jnp.float32),
            pltpu.VMEM((9, ensemble, slots), jnp.bfloat16),
            pltpu.VMEM((9, 16, ensemble), jnp.bfloat16),
            pltpu.VMEM((2, ensemble, ensemble), jnp.bfloat16),
            pltpu.VMEM((2, ensemble, ensemble), jnp.bfloat16),
            pltpu.VMEM((ensemble, ensemble), jnp.bfloat16),
            dma((5,)),
            dma((4,)),
            dma((width // LANES,)),
            dma((2,)), dma((2,)),
            dma((fields, groups, n_mem)), dma((fields, groups, n_mem)),
            dma((2, 9)), dma((2, 9)),
        ],
        compiler_params=pltpu.CompilerParams(
            collective_id=0, has_side_effects=True, vmem_limit_bytes=62 * 1024 * 1024
        ),
    )(
        ensemble_height_winds.reshape(members * fields * lines, width),
        obs_count, obs_cell, obs_value, obs_rinv,
    )
    out = pl.pallas_call(
        apply_transform,
        grid=(fields,),
        out_shape=jax.ShapeDtypeStruct((fields, ensemble, cells), jnp.float32),
        in_specs=[
            pl.BlockSpec((ensemble, ensemble), lambda f: (0, 0)),
            pl.BlockSpec((1, ensemble, cells), lambda f: (f, 0, 0)),
            pl.BlockSpec((1, 8, cells), lambda f: (f, 0, 0)),
        ],
        out_specs=pl.BlockSpec((1, ensemble, cells), lambda f: (f, 0, 0)),
    )(transform, deviations, means)
    return out.transpose(1, 0, 2)[None, None]


def solution(mesh):
    in_specs = (
        P("mem", None, "lat", None),
        P("lat", None),
        P("lat", None, None),
        P("lat", None, None),
        P("lat", None, None),
    )
    out_specs = P("lat", "mem", None, None, None)
    return jax.shard_map(
        functools.partial(per_device, mesh.shape["mem"], mesh.shape["lat"]),
        mesh=mesh, in_specs=in_specs, out_specs=out_specs, check_vma=False
    )
```

```python
import functools
import math

import jax
import jax.numpy as jnp
from jax import lax
from jax.experimental import pallas as pl
from jax.experimental.pallas import tpu as pltpu
from jax.sharding import PartitionSpec as P

PATCH_EDGE_LEN = 16
NS_ITERS = 5
GRAVITY = 1.0
DEPTH = 1.0
CORIOLIS = 0.25
TIME_STEP = 0.5
LOCALITY = (0.35, 0.6, 1.0)
NEWTON_SCALE = 16.0
HALO = 3
LANES = 128
MESH = pl.DeviceIdType.MESH


def split_rows(row):
    first = row.astype(jnp.bfloat16).astype(jnp.float32)
    second = (row - first).astype(jnp.bfloat16).astype(jnp.float32)
    third = row - first - second
    at = lax.broadcasted_iota(jnp.int32, (16, row.shape[1]), 0)
    rows = jnp.where(at == 0, first, jnp.where(at == 1, second, jnp.where(at == 2, third, 0.0)))
    return rows.astype(jnp.bfloat16)


def dot_nt(a, b):
    return lax.dot_general(a, b, (((1,), (1,)), ((), ())), preferred_element_type=jnp.float32)


def dot_nn(a, b):
    return jnp.dot(a, b, preferred_element_type=jnp.float32)


def step_row(src, row, group, cols):
    size = cols.shape[1]

    def at(field, i):
        return src[field, i, group, :]

    def dx(a):
        right = jnp.where(cols == size - 1, 0.0, pltpu.roll(a, size - 1, 1))
        left = jnp.where(cols == 0, 0.0, pltpu.roll(a, 1, 1))
        return right - left

    h, u, v = at(0, row), at(1, row), at(2, row)
    hm, um, vm = at(0, row - 1), at(1, row - 1), at(2, row - 1)
    hp, up, vp = at(0, row + 1), at(1, row + 1), at(2, row + 1)
    half = 0.5 * TIME_STEP
    turn = CORIOLIS * TIME_STEP
    new_h = h - half * (dx((DEPTH + h) * u) + ((DEPTH + hp) * vp - (DEPTH + hm) * vm))
    new_u = u - half * (u * dx(u) + v * (up - um) + GRAVITY * dx(h)) + turn * v
    new_v = v - half * (u * dx(v) + v * (vp - vm) + GRAVITY * (hp - hm)) - turn * u
    return new_h, new_u, new_v


def kernel(n_mem, n_lat, x_hbm, cnt_hbm, cell_hbm, val_hbm, rinv_hbm, mb_out, dev_out, bar_out, cnt, cell, val, rinv, xs, q, s1, s2, fin, sb, x, dev, bar, nby, nbv,
           yb, zb, mb, out_sem, obs_sem, load_sem, halo_send, halo_recv, a2a_send, a2a_recv, nb_send, nb_recv):
    me, lat = lax.axis_index("mem"), lax.axis_index("lat")
    _, rows_ext, members, width = q.shape
    lines = rows_ext - 2 * HALO
    ensemble = x.shape[1]
    group_size = min(16, members)
    groups = [pl.ds(g * group_size, group_size) for g in range(members // group_size)]

    barrier = pltpu.get_barrier_semaphore()

    loads = [
        pltpu.make_async_copy(x_hbm.at[:, pl.ds(i * LANES, LANES)], xs.at[i], load_sem.at[i])
        for i in range(width // LANES)
    ]
    for load in loads:
        load.start()
    obs_loads = [
        pltpu.make_async_copy(src, dst, obs_sem.at[i])
        for i, (src, dst) in enumerate(((cnt_hbm, cnt), (cell_hbm, cell), (val_hbm, val), (rinv_hbm, rinv)))
    ]
    for load in obs_loads:
        load.start()

    def greet(k, _):
        pl.semaphore_signal(barrier, inc=1, device_id=(lax.rem(me + k, n_mem), lat), device_id_type=MESH)
        return 0

    lax.fori_loop(1, n_mem, greet, 0)
    beside = [(p, q_) for p in (-1, 1) for q_ in (-1, 0, 1)]
    for p, q_ in beside:
        pl.semaphore_signal(
            barrier, inc=1,
            device_id=(lax.rem(me + q_ + n_mem, n_mem), lax.rem(lat + p + n_lat, n_lat)),
            device_id_type=MESH,
        )
    for load in loads:
        load.wait()
    stride = 3 * lines
    for i in range(width // LANES):
        for f in range(3):
            for r in range(lines):
                q[f, HALO + r, :, i * LANES:(i + 1) * LANES] = xs[i, pl.ds(f * lines + r, members, stride=stride), :]

    top = jnp.where(lat > 0, 1.0, 0.0)
    bottom = jnp.where(lat < n_lat - 1, 1.0, 0.0)
    cols = lax.broadcasted_iota(jnp.int32, (group_size, width), 1)

    def keep(i):
        return jnp.where(i < HALO, top, jnp.where(i >= HALO + lines, bottom, 1.0))

    def first(i, group):
        for f, new in enumerate(step_row(q, i, group, cols)):
            s1[f, i, group, :] = new * keep(i)

    def second(i, group):
        for f, new in enumerate(step_row(s1, i, group, cols)):
            s2[f, i, group, :] = (0.75 * q[f, i, group, :] + 0.25 * new) * keep(i)

    def third(i, group):
        for f, new in enumerate(step_row(s2, i, group, cols)):
            fin[f, i - HALO, group, :] = q[f, i, group, :] * (1.0 / 3.0) + (2.0 / 3.0) * new

    def over_rows(stage, low, high, group):
        def pair(i, _):
            stage(low + 2 * i, group)
            stage(low + 2 * i + 1, group)
            return 0

        lax.fori_loop(0, (high - low) // 2, pair, 0)

    per = LANES // PATCH_EDGE_LEN
    lane_group = lax.broadcasted_iota(jnp.int32, (group_size, LANES), 1) // PATCH_EDGE_LEN

    def part(f, g, k):
        target = lax.rem(me + k, n_mem)
        mine = pl.ds(pl.multiple_of(me * members + g * group_size, group_size), group_size)
        return pltpu.make_async_remote_copy(
            sb.at[target, f, groups[g]], x.at[f, mine], a2a_send.at[f, g, k], a2a_recv.at[f, g, k],
            device_id=(target, lat), device_id_type=MESH)

    def regroup(f, g):
        group = groups[g]

        def body(hb, _):
            lanes = pl.ds(pl.multiple_of(hb * LANES, LANES), LANES)
            for hr in range(lines // per):
                v = [fin[f, hr * per + i, group, lanes] for i in range(per)]
                k = per // 2
                while k:
                    high = (lane_group & k) > 0
                    for i in range(per):
                        if not i & k:
                            lo, hi = v[i], v[i + k]
                            v[i] = jnp.where(high, pltpu.roll(hi, PATCH_EDGE_LEN * k, 1), lo)
                            v[i + k] = jnp.where(high, hi, pltpu.roll(lo, LANES - PATCH_EDGE_LEN * k, 1))
                    k //= 2
                for j in range(per):
                    sb[hb * per + j, f, group, hr * LANES:(hr + 1) * LANES] = v[j].astype(sb.dtype)
            return 0

        lax.fori_loop(0, width // LANES, body, 0)

    def send(f, g):
        def one(k, _):
            part(f, g, k).start()
            return 0

        lax.fori_loop(1, n_mem, one, 0)
        x[f, pl.ds(pl.multiple_of(me * members + g * group_size, group_size), group_size), :] = sb[me, f, groups[g]]

    def arrive(f):
        def wait(k, _):
            for g in range(len(groups)):
                part(f, g, k).wait()
            return 0

        lax.fori_loop(1, n_mem, wait, 0)

    def centre(f):
        total = x[f].astype(jnp.float32)
        mean = jnp.sum(total, axis=0, keepdims=True) * (1.0 / ensemble)
        bar[f] = jnp.broadcast_to(mean, bar.shape[1:])
        dev[f] = (total - mean).astype(jnp.bfloat16)

    for group in groups:
        over_rows(first, HALO + 1, HALO + lines - 1, group)
    pl.semaphore_wait(barrier, n_mem - 1 + len(beside))

    above = (me, lax.rem(lat + n_lat - 1, n_lat))
    below = (me, lax.rem(lat + 1, n_lat))
    halos = [
        pltpu.make_async_remote_copy(
            q.at[:, pl.ds(HALO, HALO)], q.at[:, pl.ds(HALO + lines, HALO)],
            halo_send.at[0], halo_recv.at[0], device_id=above, device_id_type=MESH),
        pltpu.make_async_remote_copy(
            q.at[:, pl.ds(lines, HALO)], q.at[:, pl.ds(0, HALO)],
            halo_send.at[1], halo_recv.at[1], device_id=below, device_id_type=MESH),
    ]
    for halo in halos:
        halo.start()
    later = []
    for g, group in enumerate(groups):
        over_rows(second, HALO + 2, HALO + lines - 2, group)
        over_rows(third, HALO + 3, HALO + lines - 3, group)
        if g == 0:
            for halo in halos:
                halo.wait()
            for f in range(3):
                for r in range(HALO):
                    q[f, r] = q[f, r] * top
                    q[f, HALO + lines + r] = q[f, HALO + lines + r] * bottom
        for at, stage in enumerate((first, second, third)):
            def edge(j, _, group=group, at=at, stage=stage):
                stage(j + 1 + at, group)
                stage(j + lines + HALO - 1 - at, group)
                return 0

            lax.fori_loop(0, HALO, edge, 0)
        regroup(0, g)
        send(0, g)
        for f in (1, 2):
            regroup(f, g)
            if f == 1 and g + 1 < len(groups):
                send(f, g)
            else:
                later.append((f, g))
    for load in obs_loads:
        load.wait()

    def leave(f):
        return pltpu.make_async_copy(dev.at[f], dev_out.at[f], out_sem.at[f])

    arrive(0)
    centre(0)
    leave(0).start()

    slots = cell.shape[2]
    cells = lax.broadcasted_iota(jnp.int32, (x.shape[2], slots), 0)
    one_hot = jnp.where(cells == cell[0, pl.ds(me, 1), :], 1.0, 0.0).astype(jnp.bfloat16)
    hx = dot_nn(dev[0], one_hot)
    ybar = jnp.sum(hx, axis=0, keepdims=True) * (1.0 / ensemble)
    slot = lax.broadcasted_iota(jnp.int32, (1, slots), 1)
    count = jnp.sum(
        jnp.where(lax.broadcasted_iota(jnp.int32, cnt.shape, 1) == me, cnt[...], 0), axis=1, keepdims=True)
    weight = jnp.where(slot < count, jnp.sqrt(rinv[0, pl.ds(me, 1), :]), 0.0)
    nby[4] = (weight * (hx - ybar) / math.sqrt(ensemble - 1)).astype(jnp.bfloat16)
    misfit = weight * (val[0, pl.ds(me, 1), :] - ybar)
    summary = jnp.sum(dot_nt(split_rows(misfit), nby[4]), axis=0, keepdims=True)
    nbv[4] = jnp.broadcast_to(summary, nbv.shape[1:]).astype(jnp.bfloat16)

    def inside(p, q_):
        return (lat + p >= 0) & (lat + p < n_lat) & (me + q_ >= 0) & (me + q_ < n_mem)

    def block(p, q_, source, slot_there):
        return [
            pltpu.make_async_remote_copy(
                src.at[source], src.at[slot_there], nb_send.at[i, slot_there], nb_recv.at[i, slot_there],
                device_id=(me + q_, lat + p), device_id_type=MESH)
            for i, src in enumerate((nby, nbv))
        ]

    def across(q_):
        return block(0, q_, 4, 4 - q_)

    def along(p, c):
        return block(p, 0, 4 + c, (1 - p) * 3 + 1 + c)

    def clear(here):
        nby[here] = jnp.zeros(nby.shape[1:], jnp.bfloat16)
        nbv[here] = jnp.zeros(nbv.shape[1:], jnp.bfloat16)

    for q_ in (-1, 1):
        @pl.when(inside(0, q_))
        def _(q_=q_):
            for copy in across(q_):
                copy.start()

    for p in (-1, 1):
        @pl.when(inside(p, 0))
        def _(p=p):
            for copy in along(p, 0):
                copy.start()

    for f, g in sorted(later):
        send(f, g)

    for q_ in (-1, 1):
        @pl.when(inside(0, q_))
        def _(q_=q_):
            for copy in across(q_):
                copy.wait_send()
            for copy in block(0, q_, 4, 4 + q_):
                copy.wait_recv()

        @pl.when(jnp.logical_not(inside(0, q_)))
        def _(q_=q_):
            clear(4 + q_)

    for p in (-1, 1):
        @pl.when(inside(p, 0))
        def _(p=p):
            for c in (-1, 1):
                for copy in along(p, c):
                    copy.start()

    for p in (-1, 1):
        @pl.when(inside(p, 0))
        def _(p=p):
            for c in (-1, 0, 1):
                for copy in along(p, c):
                    copy.wait_send()
                for copy in block(p, 0, 4 + c, (1 + p) * 3 + 1 + c):
                    copy.wait_recv()

        @pl.when(jnp.logical_not(inside(p, 0)))
        def _(p=p):
            for c in (-1, 0, 1):
                clear((1 + p) * 3 + 1 + c)

    edges, corners = (1, 3, 5, 7), (0, 2, 6, 8)
    drive = nbv[4, 0:1, :].astype(jnp.float32)
    for i in edges:
        drive = drive + LOCALITY[1] * nbv[i, 0:1, :].astype(jnp.float32)
    for i in corners:
        drive = drive + LOCALITY[0] * nbv[i, 0:1, :].astype(jnp.float32)

    tile = ensemble // 2

    def eye(r):
        rows = lax.broadcasted_iota(jnp.int32, (tile, ensemble), 0) + r * tile
        return jnp.where(rows == lax.broadcasted_iota(jnp.int32, (tile, ensemble), 1), 1.0, 0.0)

    halves = [slice(r * tile, (r + 1) * tile) for r in range(2)]
    for r, at in enumerate(halves):
        gram = dot_nt(nby[4, at], nby[4])
        for w, which in ((LOCALITY[1], edges), (LOCALITY[0], corners)):
            left = jnp.concatenate([nby[i, at] for i in which], axis=1)
            gram = gram + w * dot_nt(left, jnp.concatenate([nby[i] for i in which], axis=1))
        root = ((eye(r) + gram) * (1.0 / NEWTON_SCALE)).astype(jnp.bfloat16)
        yb[0, at] = root
        mb[at] = (1.5 * eye(r) - 0.5 * root.astype(jnp.float32)).astype(jnp.bfloat16)

    for sweep in range(NS_ITERS):
        now, then = sweep % 2, (sweep + 1) % 2
        if sweep > 0:
            for r, at in enumerate(halves):
                product = dot_nn(yb[now, at], zb[now])
                mb[at] = (1.5 * eye(r) - 0.5 * product).astype(jnp.bfloat16)
        for at in halves:
            if sweep + 1 < NS_ITERS:
                yb[then, at] = dot_nn(mb[at], yb[now]).astype(jnp.bfloat16)
            if sweep > 0:
                zb[then, at] = dot_nn(zb[now, at], mb[...]).astype(jnp.bfloat16)
            else:
                zb[then, at] = mb[at]
    last = NS_ITERS % 2
    inner = jnp.sum(dot_nn(split_rows(drive), zb[last]), axis=0, keepdims=True)
    weights = jnp.sum(dot_nn(split_rows(inner), zb[last]), axis=0, keepdims=True) * (1.0 / NEWTON_SCALE)
    shift = weights * (1.0 / math.sqrt(ensemble - 1))
    mb[...] = (shift + zb[last].astype(jnp.float32) * (1.0 / math.sqrt(NEWTON_SCALE))).astype(jnp.bfloat16)

    transform_out = pltpu.make_async_copy(mb, mb_out, out_sem.at[3])
    transform_out.start()
    for f in (1, 2):
        arrive(f)
        centre(f)
        leave(f).start()
    means_out = pltpu.make_async_copy(bar, bar_out, out_sem.at[4])
    means_out.start()
    for f in range(3):
        leave(f).wait()
    transform_out.wait()
    means_out.wait()


def apply_transform(mb, dev, bar, out):
    out[0] = bar[0, 0:1, :] + dot_nn(mb[...], dev[0])


def per_device(n_mem, n_lat, ensemble_height_winds, obs_count, obs_cell, obs_value, obs_rinv):
    members, fields, lines, width = ensemble_height_winds.shape
    ensemble = members * n_mem
    cells = PATCH_EDGE_LEN * PATCH_EDGE_LEN
    slots = obs_cell.shape[2]
    link = jnp.bfloat16 if members % 16 == 0 else jnp.float32
    rows_ext = lines + 2 * HALO
    groups = members // min(16, members)
    dma = pltpu.SemaphoreType.DMA
    transform, deviations, means = pl.pallas_call(
        functools.partial(kernel, n_mem, n_lat),
        out_shape=(
            jax.ShapeDtypeStruct((ensemble, ensemble), jnp.bfloat16),
            jax.ShapeDtypeStruct((fields, ensemble, cells), jnp.bfloat16),
            jax.ShapeDtypeStruct((fields, 8, cells), jnp.float32),
        ),
        in_specs=[pl.BlockSpec(memory_space=pltpu.HBM)] * 5,
        out_specs=[pl.BlockSpec(memory_space=pltpu.HBM)] * 3,
        scratch_shapes=[
            *(pltpu.VMEM(a.shape, a.dtype) for a in (obs_count, obs_cell, obs_value, obs_rinv)),
            pltpu.VMEM((width // LANES, members * fields * lines, LANES), jnp.float32),
            pltpu.VMEM((fields, rows_ext, members, width), jnp.float32),
            pltpu.VMEM((fields, rows_ext, members, width), jnp.float32),
            pltpu.VMEM((fields, rows_ext, members, width), jnp.float32),
            pltpu.VMEM((fields, lines, members, width), jnp.float32),
            pltpu.VMEM((n_mem, fields, members, cells), link),
            pltpu.VMEM((fields, ensemble, cells), link),
            pltpu.VMEM((fields, ensemble, cells), jnp.bfloat16),
            pltpu.VMEM((fields, 8, cells), jnp.float32),
            pltpu.VMEM((9, ensemble, slots), jnp.bfloat16),
            pltpu.VMEM((9, 16, ensemble), jnp.bfloat16),
            pltpu.VMEM((2, ensemble, ensemble), jnp.bfloat16),
            pltpu.VMEM((2, ensemble, ensemble), jnp.bfloat16),
            pltpu.VMEM((ensemble, ensemble), jnp.bfloat16),
            dma((5,)),
            dma((4,)),
            dma((width // LANES,)),
            dma((2,)), dma((2,)),
            dma((fields, groups, n_mem)), dma((fields, groups, n_mem)),
            dma((2, 9)), dma((2, 9)),
        ],
        compiler_params=pltpu.CompilerParams(
            collective_id=0, has_side_effects=True, vmem_limit_bytes=62 * 1024 * 1024
        ),
    )(
        ensemble_height_winds.reshape(members * fields * lines, width),
        obs_count, obs_cell, obs_value, obs_rinv,
    )
    out = pl.pallas_call(
        apply_transform,
        grid=(fields,),
        out_shape=jax.ShapeDtypeStruct((fields, ensemble, cells), jnp.float32),
        in_specs=[
            pl.BlockSpec((ensemble, ensemble), lambda f: (0, 0)),
            pl.BlockSpec((1, ensemble, cells), lambda f: (f, 0, 0)),
            pl.BlockSpec((1, 8, cells), lambda f: (f, 0, 0)),
        ],
        out_specs=pl.BlockSpec((1, ensemble, cells), lambda f: (f, 0, 0)),
    )(transform, deviations, means)
    return out.transpose(1, 0, 2)[None, None]


def solution(mesh):
    in_specs = (
        P("mem", None, "lat", None),
        P("lat", None),
        P("lat", None, None),
        P("lat", None, None),
        P("lat", None, None),
    )
    out_specs = P("lat", "mem", None, None, None)
    return jax.shard_map(
        functools.partial(per_device, mesh.shape["mem"], mesh.shape["lat"]),
        mesh=mesh, in_specs=in_specs, out_specs=out_specs, check_vma=False
    )
```

```python
import functools
import math

import jax
import jax.numpy as jnp
from jax import lax
from jax.experimental import pallas as pl
from jax.experimental.pallas import tpu as pltpu
from jax.sharding import PartitionSpec as P

PATCH_EDGE_LEN = 16
NS_ITERS = 5
GRAVITY = 1.0
DEPTH = 1.0
CORIOLIS = 0.25
TIME_STEP = 0.5
LOCALITY = (0.35, 0.6, 1.0)
NEWTON_SCALE = 16.0
HALO = 3
LANES = 128
MESH = pl.DeviceIdType.MESH


def split_rows(row):
    first = row.astype(jnp.bfloat16).astype(jnp.float32)
    second = (row - first).astype(jnp.bfloat16).astype(jnp.float32)
    third = row - first - second
    at = lax.broadcasted_iota(jnp.int32, (16, row.shape[1]), 0)
    rows = jnp.where(at == 0, first, jnp.where(at == 1, second, jnp.where(at == 2, third, 0.0)))
    return rows.astype(jnp.bfloat16)


def dot_nt(a, b):
    return lax.dot_general(a, b, (((1,), (1,)), ((), ())), preferred_element_type=jnp.float32)


def dot_nn(a, b):
    return jnp.dot(a, b, preferred_element_type=jnp.float32)


def step_row(src, row, group, cols):
    size = cols.shape[1]

    def at(field, i):
        return src[field, i, group, :]

    def dx(a):
        right = jnp.where(cols == size - 1, 0.0, pltpu.roll(a, size - 1, 1))
        left = jnp.where(cols == 0, 0.0, pltpu.roll(a, 1, 1))
        return right - left

    h, u, v = at(0, row), at(1, row), at(2, row)
    hm, um, vm = at(0, row - 1), at(1, row - 1), at(2, row - 1)
    hp, up, vp = at(0, row + 1), at(1, row + 1), at(2, row + 1)
    half = 0.5 * TIME_STEP
    turn = CORIOLIS * TIME_STEP
    new_h = h - half * (dx((DEPTH + h) * u) + ((DEPTH + hp) * vp - (DEPTH + hm) * vm))
    new_u = u - half * (u * dx(u) + v * (up - um) + GRAVITY * dx(h)) + turn * v
    new_v = v - half * (u * dx(v) + v * (vp - vm) + GRAVITY * (hp - hm)) - turn * u
    return new_h, new_u, new_v


def kernel(n_mem, n_lat, x_hbm, cnt_hbm, cell_hbm, val_hbm, rinv_hbm, out_hbm, cnt, cell, val, rinv, xs, q, s1, s2, fin, sb, x, dev, bar, nby, nbv,
           yb, zb, mb, out, out_sem, obs_sem, load_sem, halo_send, halo_recv, a2a_send, a2a_recv, nb_send, nb_recv):
    me, lat = lax.axis_index("mem"), lax.axis_index("lat")
    _, rows_ext, members, width = q.shape
    lines = rows_ext - 2 * HALO
    ensemble = x.shape[1]
    group_size = min(16, members)
    groups = [pl.ds(g * group_size, group_size) for g in range(members // group_size)]

    barrier = pltpu.get_barrier_semaphore()

    loads = [
        pltpu.make_async_copy(x_hbm.at[:, pl.ds(i * LANES, LANES)], xs.at[i], load_sem.at[i])
        for i in range(width // LANES)
    ]
    for load in loads:
        load.start()
    obs_loads = [
        pltpu.make_async_copy(src, dst, obs_sem.at[i])
        for i, (src, dst) in enumerate(((cnt_hbm, cnt), (cell_hbm, cell), (val_hbm, val), (rinv_hbm, rinv)))
    ]
    for load in obs_loads:
        load.start()

    def greet(k, _):
        pl.semaphore_signal(barrier, inc=1, device_id=(lax.rem(me + k, n_mem), lat), device_id_type=MESH)
        return 0

    lax.fori_loop(1, n_mem, greet, 0)
    beside = [(p, q_) for p in (-1, 1) for q_ in (-1, 0, 1)]
    for p, q_ in beside:
        pl.semaphore_signal(
            barrier, inc=1,
            device_id=(lax.rem(me + q_ + n_mem, n_mem), lax.rem(lat + p + n_lat, n_lat)),
            device_id_type=MESH,
        )
    for load in loads:
        load.wait()
    stride = 3 * lines
    for i in range(width // LANES):
        for f in range(3):
            for r in range(lines):
                q[f, HALO + r, :, i * LANES:(i + 1) * LANES] = xs[i, pl.ds(f * lines + r, members, stride=stride), :]

    top = jnp.where(lat > 0, 1.0, 0.0)
    bottom = jnp.where(lat < n_lat - 1, 1.0, 0.0)
    cols = lax.broadcasted_iota(jnp.int32, (group_size, width), 1)

    def keep(i):
        return jnp.where(i < HALO, top, jnp.where(i >= HALO + lines, bottom, 1.0))

    def first(i, group):
        for f, new in enumerate(step_row(q, i, group, cols)):
            s1[f, i, group, :] = new * keep(i)

    def second(i, group):
        for f, new in enumerate(step_row(s1, i, group, cols)):
            s2[f, i, group, :] = (0.75 * q[f, i, group, :] + 0.25 * new) * keep(i)

    def third(i, group):
        for f, new in enumerate(step_row(s2, i, group, cols)):
            fin[f, i - HALO, group, :] = q[f, i, group, :] * (1.0 / 3.0) + (2.0 / 3.0) * new

    def over_rows(stage, low, high, group):
        def pair(i, _):
            stage(low + 2 * i, group)
            stage(low + 2 * i + 1, group)
            return 0

        lax.fori_loop(0, (high - low) // 2, pair, 0)

    per = LANES // PATCH_EDGE_LEN
    lane_group = lax.broadcasted_iota(jnp.int32, (group_size, LANES), 1) // PATCH_EDGE_LEN

    def part(f, g, k):
        target = lax.rem(me + k, n_mem)
        mine = pl.ds(pl.multiple_of(me * members + g * group_size, group_size), group_size)
        return pltpu.make_async_remote_copy(
            sb.at[target, f, groups[g]], x.at[f, mine], a2a_send.at[f, g, k], a2a_recv.at[f, g, k],
            device_id=(target, lat), device_id_type=MESH)

    def regroup(f, g):
        group = groups[g]

        def body(hb, _):
            lanes = pl.ds(pl.multiple_of(hb * LANES, LANES), LANES)
            for hr in range(lines // per):
                v = [fin[f, hr * per + i, group, lanes] for i in range(per)]
                k = per // 2
                while k:
                    high = (lane_group & k) > 0
                    for i in range(per):
                        if not i & k:
                            lo, hi = v[i], v[i + k]
                            v[i] = jnp.where(high, pltpu.roll(hi, PATCH_EDGE_LEN * k, 1), lo)
                            v[i + k] = jnp.where(high, hi, pltpu.roll(lo, LANES - PATCH_EDGE_LEN * k, 1))
                    k //= 2
                for j in range(per):
                    sb[hb * per + j, f, group, hr * LANES:(hr + 1) * LANES] = v[j].astype(sb.dtype)
            return 0

        lax.fori_loop(0, width // LANES, body, 0)

    def send(f, g):
        def one(k, _):
            part(f, g, k).start()
            return 0

        lax.fori_loop(1, n_mem, one, 0)
        x[f, pl.ds(pl.multiple_of(me * members + g * group_size, group_size), group_size), :] = sb[me, f, groups[g]]

    def arrive(f):
        def wait(k, _):
            for g in range(len(groups)):
                part(f, g, k).wait()
            return 0

        lax.fori_loop(1, n_mem, wait, 0)

    def centre(f):
        total = x[f].astype(jnp.float32)
        mean = jnp.sum(total, axis=0, keepdims=True) * (1.0 / ensemble)
        bar[f] = jnp.broadcast_to(mean, bar.shape[1:])
        dev[f] = (total - mean).astype(jnp.bfloat16)

    for group in groups:
        over_rows(first, HALO + 1, HALO + lines - 1, group)
    pl.semaphore_wait(barrier, n_mem - 1 + len(beside))

    above = (me, lax.rem(lat + n_lat - 1, n_lat))
    below = (me, lax.rem(lat + 1, n_lat))
    halos = [
        pltpu.make_async_remote_copy(
            q.at[:, pl.ds(HALO, HALO)], q.at[:, pl.ds(HALO + lines, HALO)],
            halo_send.at[0], halo_recv.at[0], device_id=above, device_id_type=MESH),
        pltpu.make_async_remote_copy(
            q.at[:, pl.ds(lines, HALO)], q.at[:, pl.ds(0, HALO)],
            halo_send.at[1], halo_recv.at[1], device_id=below, device_id_type=MESH),
    ]
    for halo in halos:
        halo.start()
    later = []
    for g, group in enumerate(groups):
        over_rows(second, HALO + 2, HALO + lines - 2, group)
        over_rows(third, HALO + 3, HALO + lines - 3, group)
        if g == 0:
            for halo in halos:
                halo.wait()
            for f in range(3):
                for r in range(HALO):
                    q[f, r] = q[f, r] * top
                    q[f, HALO + lines + r] = q[f, HALO + lines + r] * bottom
        for at, stage in enumerate((first, second, third)):
            def edge(j, _, group=group, at=at, stage=stage):
                stage(j + 1 + at, group)
                stage(j + lines + HALO - 1 - at, group)
                return 0

            lax.fori_loop(0, HALO, edge, 0)
        regroup(0, g)
        send(0, g)
        for f in (1, 2):
            regroup(f, g)
            if f == 1 and g + 1 < len(groups):
                send(f, g)
            else:
                later.append((f, g))
    for load in obs_loads:
        load.wait()

    def leave(f):
        return pltpu.make_async_copy(out.at[f], out_hbm.at[f], out_sem.at[f])

    arrive(0)
    centre(0)

    slots = cell.shape[2]
    cells = lax.broadcasted_iota(jnp.int32, (x.shape[2], slots), 0)
    one_hot = jnp.where(cells == cell[0, pl.ds(me, 1), :], 1.0, 0.0).astype(jnp.bfloat16)
    hx = dot_nn(dev[0], one_hot)
    ybar = jnp.sum(hx, axis=0, keepdims=True) * (1.0 / ensemble)
    slot = lax.broadcasted_iota(jnp.int32, (1, slots), 1)
    count = jnp.sum(
        jnp.where(lax.broadcasted_iota(jnp.int32, cnt.shape, 1) == me, cnt[...], 0), axis=1, keepdims=True)
    weight = jnp.where(slot < count, jnp.sqrt(rinv[0, pl.ds(me, 1), :]), 0.0)
    nby[4] = (weight * (hx - ybar) / math.sqrt(ensemble - 1)).astype(jnp.bfloat16)
    misfit = weight * (val[0, pl.ds(me, 1), :] - ybar)
    summary = jnp.sum(dot_nt(split_rows(misfit), nby[4]), axis=0, keepdims=True)
    nbv[4] = jnp.broadcast_to(summary, nbv.shape[1:]).astype(jnp.bfloat16)

    def inside(p, q_):
        return (lat + p >= 0) & (lat + p < n_lat) & (me + q_ >= 0) & (me + q_ < n_mem)

    def block(p, q_, source, slot_there):
        return [
            pltpu.make_async_remote_copy(
                src.at[source], src.at[slot_there], nb_send.at[i, slot_there], nb_recv.at[i, slot_there],
                device_id=(me + q_, lat + p), device_id_type=MESH)
            for i, src in enumerate((nby, nbv))
        ]

    def across(q_):
        return block(0, q_, 4, 4 - q_)

    def along(p, c):
        return block(p, 0, 4 + c, (1 - p) * 3 + 1 + c)

    def clear(here):
        nby[here] = jnp.zeros(nby.shape[1:], jnp.bfloat16)
        nbv[here] = jnp.zeros(nbv.shape[1:], jnp.bfloat16)

    for q_ in (-1, 1):
        @pl.when(inside(0, q_))
        def _(q_=q_):
            for copy in across(q_):
                copy.start()

    for p in (-1, 1):
        @pl.when(inside(p, 0))
        def _(p=p):
            for copy in along(p, 0):
                copy.start()

    for f, g in sorted(later):
        send(f, g)

    for q_ in (-1, 1):
        @pl.when(inside(0, q_))
        def _(q_=q_):
            for copy in across(q_):
                copy.wait_send()
            for copy in block(0, q_, 4, 4 + q_):
                copy.wait_recv()

        @pl.when(jnp.logical_not(inside(0, q_)))
        def _(q_=q_):
            clear(4 + q_)

    for p in (-1, 1):
        @pl.when(inside(p, 0))
        def _(p=p):
            for c in (-1, 1):
                for copy in along(p, c):
                    copy.start()

    for p in (-1, 1):
        @pl.when(inside(p, 0))
        def _(p=p):
            for c in (-1, 0, 1):
                for copy in along(p, c):
                    copy.wait_send()
                for copy in block(p, 0, 4 + c, (1 + p) * 3 + 1 + c):
                    copy.wait_recv()

        @pl.when(jnp.logical_not(inside(p, 0)))
        def _(p=p):
            for c in (-1, 0, 1):
                clear((1 + p) * 3 + 1 + c)

    edges, corners = (1, 3, 5, 7), (0, 2, 6, 8)
    drive = nbv[4, 0:1, :].astype(jnp.float32)
    for i in edges:
        drive = drive + LOCALITY[1] * nbv[i, 0:1, :].astype(jnp.float32)
    for i in corners:
        drive = drive + LOCALITY[0] * nbv[i, 0:1, :].astype(jnp.float32)

    tile = ensemble // 2

    def eye(r):
        rows = lax.broadcasted_iota(jnp.int32, (tile, ensemble), 0) + r * tile
        return jnp.where(rows == lax.broadcasted_iota(jnp.int32, (tile, ensemble), 1), 1.0, 0.0)

    halves = [slice(r * tile, (r + 1) * tile) for r in range(2)]
    for r, at in enumerate(halves):
        gram = dot_nt(nby[4, at], nby[4])
        for w, which in ((LOCALITY[1], edges), (LOCALITY[0], corners)):
            left = jnp.concatenate([nby[i, at] for i in which], axis=1)
            gram = gram + w * dot_nt(left, jnp.concatenate([nby[i] for i in which], axis=1))
        root = ((eye(r) + gram) * (1.0 / NEWTON_SCALE)).astype(jnp.bfloat16)
        yb[0, at] = root
        mb[at] = (1.5 * eye(r) - 0.5 * root.astype(jnp.float32)).astype(jnp.bfloat16)

    for sweep in range(NS_ITERS):
        now, then = sweep % 2, (sweep + 1) % 2
        if sweep > 0:
            for r, at in enumerate(halves):
                product = dot_nn(yb[now, at], zb[now])
                mb[at] = (1.5 * eye(r) - 0.5 * product).astype(jnp.bfloat16)
        for at in halves:
            if sweep + 1 < NS_ITERS:
                yb[then, at] = dot_nn(mb[at], yb[now]).astype(jnp.bfloat16)
            if sweep > 0:
                zb[then, at] = dot_nn(zb[now, at], mb[...]).astype(jnp.bfloat16)
            else:
                zb[then, at] = mb[at]
    last = NS_ITERS % 2
    inner = jnp.sum(dot_nn(split_rows(drive), zb[last]), axis=0, keepdims=True)
    weights = jnp.sum(dot_nn(split_rows(inner), zb[last]), axis=0, keepdims=True) * (1.0 / NEWTON_SCALE)
    shift = weights * (1.0 / math.sqrt(ensemble - 1))
    mb[...] = (shift + zb[last].astype(jnp.float32) * (1.0 / math.sqrt(NEWTON_SCALE))).astype(jnp.bfloat16)

    for f in range(3):
        if f > 0:
            arrive(f)
            centre(f)
        out[f] = bar[f, 0:1, :] + dot_nn(mb[...], dev[f])
        leave(f).start()
    for f in range(3):
        leave(f).wait()


def per_device(n_mem, n_lat, ensemble_height_winds, obs_count, obs_cell, obs_value, obs_rinv):
    members, fields, lines, width = ensemble_height_winds.shape
    ensemble = members * n_mem
    cells = PATCH_EDGE_LEN * PATCH_EDGE_LEN
    slots = obs_cell.shape[2]
    link = jnp.bfloat16 if members % 16 == 0 else jnp.float32
    rows_ext = lines + 2 * HALO
    groups = members // min(16, members)
    dma = pltpu.SemaphoreType.DMA
    out = pl.pallas_call(
        functools.partial(kernel, n_mem, n_lat),
        out_shape=jax.ShapeDtypeStruct((fields, ensemble, cells), jnp.float32),
        in_specs=[pl.BlockSpec(memory_space=pltpu.HBM)] * 5,
        out_specs=pl.BlockSpec(memory_space=pltpu.HBM),
        scratch_shapes=[
            *(pltpu.VMEM(a.shape, a.dtype) for a in (obs_count, obs_cell, obs_value, obs_rinv)),
            pltpu.VMEM((width // LANES, members * fields * lines, LANES), jnp.float32),
            pltpu.VMEM((fields, rows_ext, members, width), jnp.float32),
            pltpu.VMEM((fields, rows_ext, members, width), jnp.float32),
            pltpu.VMEM((fields, rows_ext, members, width), jnp.float32),
            pltpu.VMEM((fields, lines, members, width), jnp.float32),
            pltpu.VMEM((n_mem, fields, members, cells), link),
            pltpu.VMEM((fields, ensemble, cells), link),
            pltpu.VMEM((fields, ensemble, cells), jnp.bfloat16),
            pltpu.VMEM((fields, 8, cells), jnp.float32),
            pltpu.VMEM((9, ensemble, slots), jnp.bfloat16),
            pltpu.VMEM((9, 16, ensemble), jnp.bfloat16),
            pltpu.VMEM((2, ensemble, ensemble), jnp.bfloat16),
            pltpu.VMEM((2, ensemble, ensemble), jnp.bfloat16),
            pltpu.VMEM((ensemble, ensemble), jnp.bfloat16),
            pltpu.VMEM((fields, ensemble, cells), jnp.float32),
            dma((3,)),
            dma((4,)),
            dma((width // LANES,)),
            dma((2,)), dma((2,)),
            dma((fields, groups, n_mem)), dma((fields, groups, n_mem)),
            dma((2, 9)), dma((2, 9)),
        ],
        compiler_params=pltpu.CompilerParams(
            collective_id=0, has_side_effects=True, vmem_limit_bytes=62 * 1024 * 1024
        ),
    )(
        ensemble_height_winds.reshape(members * fields * lines, width),
        obs_count, obs_cell, obs_value, obs_rinv,
    )
    return out.transpose(1, 0, 2)[None, None]


def solution(mesh):
    in_specs = (
        P("mem", None, "lat", None),
        P("lat", None),
        P("lat", None, None),
        P("lat", None, None),
        P("lat", None, None),
    )
    out_specs = P("lat", "mem", None, None, None)
    return jax.shard_map(
        functools.partial(per_device, mesh.shape["mem"], mesh.shape["lat"]),
        mesh=mesh, in_specs=in_specs, out_specs=out_specs, check_vma=False
    )
```
